512 devices in a mesh: seq: 64 (over y, z), mlp: 8 (over x, core).
Axes of the slice: x: 4, y: 8, z: 8, core: 2. Of those that a mesh axis runs over, the one named last changes fastest.
Arguments:
- queries: bfloat16 [16384, 3072], P('seq', 'mlp'), may hold values from -5 to 5
- key_vectors: bfloat16 [16384, 3072], P('seq', 'mlp'), may hold values from -5 to 5
- value_vectors: bfloat16 [16384, 3072], P('seq', 'mlp'), may hold values from -6 to 6
- head_kinds: int32 [24], P('mlp'), may hold values from 0 to 1
- block_masks: int32 [24, 2, 2], P('mlp'), may hold values from 0 to 1, as said below
- order_map: int32 [256], replicated, may hold values from 0 to 255, as said below
- out_weight: bfloat16 [3072, 3072], P('seq', 'mlp'), may hold values from -0.109375 to 0.109375
- gate_values: float32 [3072], P('mlp'), may hold values from 0.5 to 2
Outputs:
- gated_output: bfloat16 [16384, 3072], P('seq', 'mlp')
The draws below stay inside these ranges and needn't reach their ends.
Inputs may be any that keep to these rules, and one draw needn't show every extreme that they name: block_masks[h, b, b] = 1 for every head h and block b. A permutation of the 256 positions in which order_map[2 i] is even and order_map[2 i + 1] = order_map[2 i] + 1.
All inputs are finite; a program needn't handle non-finite values.
Results may differ from the reference program's by a relative error of at most 0.0056.
Values may be sent and summed in bfloat16 or wider, within the bound.
No kernel may reach another device: no remote copies, remote signals or barrier semaphores. Data moves between devices by JAX's collectives and lax.ppermute only.
A program may use at most 64 MiB of HBM per device.

```python
import math
import jax
import jax.numpy as jnp
from jax import lax

D = 3072
HEADS = 24
HD = 128
BLOCK = 128
POS = 256
FRAMES = 64
TOKENS = 16384
BLOCKS = 2
GROUP = 4


def draw_queries(key, part):
    key = jax.random.fold_in(key, 5)
    first_key = jax.random.fold_in(key, 0)
    values_base = jax.random.normal(first_key, (TOKENS, HEADS * HD), jnp.float32) * 0.35
    return jnp.clip(values_base, -5.0, 5.0).astype(jnp.bfloat16)


def draw_key_vectors(key, part):
    key = jax.random.fold_in(key, 7)
    first_key = jax.random.fold_in(key, 0)
    values_base = jax.random.normal(first_key, (TOKENS, HEADS * HD), jnp.float32) * 0.35
    return jnp.clip(values_base, -5.0, 5.0).astype(jnp.bfloat16)


def draw_block_masks(key, part):
    key = jax.random.fold_in(key, 11)
    first_key, second_key = jax.random.split(key)
    density = jax.random.randint(first_key, (HEADS, 1, 1), 2, 10)
    rolled = jax.random.randint(second_key, (HEADS, BLOCKS, BLOCKS), 0, 10)
    diagonal = jnp.eye(BLOCKS, dtype=jnp.int32)[None, :, :]
    return jnp.maximum((rolled < density).astype(jnp.int32), diagonal)


def draw_order_map(key, part):
    key = jax.random.fold_in(key, 13)
    pair_order = jax.random.permutation(key, POS // 2).astype(jnp.int32)
    return jnp.stack([2 * pair_order, 2 * pair_order + 1], axis=1).reshape(POS).astype(jnp.int32)


def with_ends(values, rng, low, top_value):
    shape = values.shape
    place = [jax.random.randint(jax.random.fold_in(rng, axis), (), 0, shape[axis]) for axis in range(len(shape))]
    values = values.at[tuple(place)].set(low)
    longest = shape.index(max(shape))
    place[longest] = (place[longest] + 1) % shape[longest]
    return values.at[tuple(place)].set(top_value)


def block_levels(key, shape, pieces, smallest, top_value):
    level = 1.0
    for dim, shards_of in pieces:
        heights = jax.random.uniform(jax.random.fold_in(jax.random.fold_in(key, 6), dim), (shards_of,), jnp.float32, smallest / len(pieces), top_value / len(pieces))
        level = level * jnp.repeat(jnp.exp(heights), shape[dim] // shards_of).reshape((-1,) + (1,) * (len(shape) - 1 - dim))
    return level


def scatter_about(own_key, shape, scale, bound, cuts=(), held_as=jnp.bfloat16):
    values = jax.random.normal(own_key, shape, jnp.float32) * scale
    if len(cuts) > 0:
        values = block_levels(own_key, shape, cuts, -0.22, 0.18) * values
    return jnp.clip(values, min=-bound, max=bound).astype(held_as)


def setup_inputs(seed: int = 0) -> dict:
    seeds = jax.random.split(jax.random.key(seed), 9)
    queries = draw_queries(jax.random.fold_in(seeds[8], 71), 0)
    key_vectors = draw_key_vectors(jax.random.fold_in(seeds[8], 71), 0)
    value_vectors = scatter_about(seeds[2], (TOKENS, HEADS * HD), 1.0, 6.0, ((0, 64), (1, 8)))
    head_kinds = with_ends(jax.random.randint(seeds[3], (HEADS,), 0, 2), jax.random.fold_in(seeds[3], 1), 0, 1).astype(jnp.int32)
    block_masks = draw_block_masks(jax.random.fold_in(seeds[8], 71), 0)
    order_map = draw_order_map(jax.random.fold_in(seeds[8], 71), 0)
    out_weight = scatter_about(seeds[6], (HEADS * HD, D), (HEADS * HD) ** -0.5, 0.109375, ((0, 64), (1, 8)))
    gate_values = jnp.clip(0.5 + 1.5 * jax.random.uniform(seeds[7], (D,), jnp.float32) ** block_levels(seeds[7], (D,), ((0, 8),), -0.2, 0.2), 0.5, 2.0)
    return {"queries": queries, "key_vectors": key_vectors, "value_vectors": value_vectors, "head_kinds": head_kinds, "block_masks": block_masks, "order_map": order_map, "out_weight": out_weight, "gate_values": gate_values}


def attend_group(query_rows, key_rows, value_rows, visible):
    score_scale = 1.0 / math.sqrt(HD)
    scores = jnp.dot(query_rows.astype(jnp.float32), key_rows.astype(jnp.float32).T, precision=lax.Precision.HIGHEST) * score_scale
    masked = jnp.where(visible, scores, -jnp.inf)
    row_max = lax.optimization_barrier(jnp.max(masked, axis=1, keepdims=True))
    weights = jnp.where(visible, jnp.exp(scores - row_max), 0.0)
    row_total = lax.optimization_barrier(jnp.sum(weights, axis=1, keepdims=True))
    rounded = lax.optimization_barrier(weights.astype(jnp.bfloat16))
    combined = jnp.dot(rounded.astype(jnp.float32), value_rows.astype(jnp.float32), precision=lax.Precision.HIGHEST)
    return (combined / row_total).astype(jnp.bfloat16)

def reference(queries, key_vectors, value_vectors, head_kinds, block_masks, order_map, out_weight, gate_values):
    spatial = jnp.arange(TOKENS, dtype=jnp.int32)
    slot_table = order_map.reshape(FRAMES, GROUP).astype(jnp.int32)
    frame_starts = jnp.arange(FRAMES, dtype=jnp.int32) * POS
    temporal = (frame_starts[None, None, :] + slot_table[:, :, None]).reshape(TOKENS).astype(jnp.int32)

    def one_head(head_index):
        layout = jnp.where(head_kinds[head_index] == 1, temporal, spatial)
        column_start = (head_index * HD).astype(jnp.int32)
        query_rows = lax.dynamic_slice_in_dim(queries, column_start, HD, 1)[layout].reshape(FRAMES, POS, HD)
        key_rows = lax.dynamic_slice_in_dim(key_vectors, column_start, HD, 1)[layout].reshape(FRAMES, POS, HD)
        value_rows = lax.dynamic_slice_in_dim(value_vectors, column_start, HD, 1)[layout].reshape(FRAMES, POS, HD)
        head_mask = block_masks[head_index] == 1
        visible = jnp.repeat(jnp.repeat(head_mask, BLOCK, axis=0), BLOCK, axis=1)

        def one_group(triple):
            return attend_group(triple[0], triple[1], triple[2], visible)
        results = lax.map(one_group, (query_rows, key_rows, value_rows))
        return jnp.zeros((TOKENS, HD), jnp.bfloat16).at[layout].set(results.reshape(TOKENS, HD))
    per_head = lax.map(one_head, jnp.arange(HEADS, dtype=jnp.int32))
    attended = jnp.transpose(per_head, (1, 0, 2)).reshape(TOKENS, HEADS * HD)
    projected = jnp.dot(attended, out_weight, preferred_element_type=jnp.float32)
    return (gate_values[None, :] * projected).astype(jnp.bfloat16)
```

```python
import functools
import math

import jax
import jax.numpy as jnp
from jax import lax
from jax.experimental import pallas as pl
from jax.experimental.pallas import tpu as pltpu
from jax.sharding import PartitionSpec as P

VMEM = pl.BlockSpec(memory_space=pltpu.VMEM)
SMEM = pl.BlockSpec(memory_space=pltpu.SMEM)
PARAMS = pltpu.CompilerParams(vmem_limit_bytes=40 * 1024 * 1024)


def placement(order, rows):
    positions = lax.broadcasted_iota(jnp.int32, (rows, rows), 0)
    return (positions == order).astype(jnp.float32).astype(jnp.bfloat16)


def send_kernel(order_ref, q_ref, k_ref, v_ref, out_ref):
    rows, width = q_ref.shape
    onehot = placement(order_ref[...], rows)
    for i, ref in enumerate((q_ref, k_ref, v_ref)):
        picked = lax.dot_general(
            onehot, ref[...], (((0,), (0,)), ((), ())), preferred_element_type=jnp.float32
        )
        out_ref[:, :, i * width : (i + 1) * width] = picked.reshape(
            out_ref.shape[0], out_ref.shape[1], width
        ).astype(jnp.bfloat16)


def attend(q, k, v, masks, head, row_block, column_block):
    depth = q.shape[1]
    scores = lax.dot_general(q, k, (((1,), (1,)), ((), ())), preferred_element_type=jnp.float32)
    scores = scores * (1.0 / math.sqrt(depth))
    seen = [masks[4 * head + i] for i in range(4)]
    chosen = jnp.where(
        row_block == 0,
        jnp.where(column_block == 0, seen[0], seen[1]),
        jnp.where(column_block == 0, seen[2], seen[3]),
    )
    visible = chosen == 1
    scores = jnp.where(visible, scores, -jnp.inf)
    row_max = jnp.max(scores, axis=1, keepdims=True)
    weights = jnp.exp(scores - row_max)
    total = jnp.sum(weights, axis=1, keepdims=True)
    combined = jnp.dot(weights.astype(jnp.bfloat16), v, preferred_element_type=jnp.float32)
    return combined / total


def near_kernel(masks_ref, q_ref, k_ref, v_ref, out_ref):
    rows, width = q_ref.shape
    heads = masks_ref.shape[0] // 4
    depth = width // heads
    row_block = lax.broadcasted_iota(jnp.int32, (rows, rows), 0) // (rows // 2)
    column_block = lax.broadcasted_iota(jnp.int32, (rows, rows), 1) // (rows // 2)
    for h in range(heads):
        c = slice(h * depth, (h + 1) * depth)
        out_ref[:, c] = attend(
            q_ref[:, c], k_ref[:, c], v_ref[:, c], masks_ref, h, row_block, column_block
        ).astype(jnp.bfloat16)


def far_kernel(masks_ref, x_ref, out_ref):
    frames, group, wide = x_ref.shape
    rows, width = frames * group, wide // 3
    heads = masks_ref.shape[0] // 4
    depth = width // heads
    row_block = (lax.broadcasted_iota(jnp.int32, (rows, rows), 0) % group) // (group // 2)
    column_block = (lax.broadcasted_iota(jnp.int32, (rows, rows), 1) % group) // (group // 2)
    for h in range(heads):
        q, k, v = (
            x_ref[:, :, i * width + h * depth : i * width + (h + 1) * depth]
            .astype(jnp.float32)
            .reshape(rows, depth)
            .astype(jnp.bfloat16)
            for i in range(3)
        )
        out = attend(q, k, v, masks_ref, h, row_block, column_block)
        out_ref[:, :, h * depth : (h + 1) * depth] = out.reshape(frames, group, depth).astype(
            jnp.bfloat16
        )


def select_kernel(kinds_ref, order_ref, far_ref, near_ref, out_ref):
    rows, width = near_ref.shape
    heads = kinds_ref.shape[0]
    depth = width // heads
    onehot = placement(order_ref[...], rows)
    for h in range(heads):
        c = slice(h * depth, (h + 1) * depth)
        far = far_ref[:, :, c].astype(jnp.float32).reshape(rows, depth).astype(jnp.bfloat16)
        back = jnp.dot(onehot, far, preferred_element_type=jnp.float32)
        near = near_ref[:, c].astype(jnp.float32)
        chosen = jnp.where(kinds_ref[h] == 1, back, near).astype(jnp.bfloat16)
        for m in range(out_ref.shape[0]):
            out_ref[m, :, c] = chosen


def order_kernel(*refs):
    *blocks, out_ref = refs
    z = lax.axis_index("seq") % 8
    for offset, rows, ref in zip((0, -1, 1, -4, 2), (48, 48, 48, 144, 96), blocks, strict=True):
        for i in range(rows // 48):
            at = lax.rem(z + (offset + i + 8), 8) * 48
            out_ref[pl.ds(pl.multiple_of(at, 16), 48), :] = ref[i * 48 : (i + 1) * 48, :]


def project_kernel(offsets, gate_ref, x_ref, *refs):
    *blocks, out_ref = refs
    n = x_ref.shape[0]
    y = lax.axis_index("seq") // n
    total = None
    for offset, w_ref in zip(offsets, blocks, strict=True):
        part = jnp.dot(
            x_ref[lax.rem(y + (offset + n), n)], w_ref[...], preferred_element_type=jnp.float32
        )
        total = part if total is None else total + part
    out_ref[...] = (gate_ref[...] * total).astype(jnp.bfloat16)


def call(kernel, shape, specs, *args):
    return pl.pallas_call(
        kernel,
        out_shape=jax.ShapeDtypeStruct(shape, jnp.bfloat16),
        in_specs=specs,
        out_specs=VMEM,
        compiler_params=PARAMS,
    )(*args)


def gather_weight(out_weight):
    def along_z(block, step):
        return lax.ppermute(
            block, "seq", [(i, i // 8 * 8 + (i + step) % 8) for i in range(64)]
        )

    def along_y(block, step):
        return lax.ppermute(block, "seq", [(i, (i + 8 * step) % 64) for i in range(64)])

    before = along_z(out_weight, 1)
    after = along_z(out_weight, -1)
    two = jnp.concatenate([before, out_weight], axis=0)
    three = jnp.concatenate([before, out_weight, after], axis=0)
    far_before = along_z(three, 3)
    far_after = along_z(two, -3)
    own = call(
        order_kernel,
        (384, out_weight.shape[1]),
        [VMEM] * 5,
        out_weight,
        before,
        after,
        far_before,
        far_after,
    )
    offsets, blocks = [0], [own]
    up = down = own
    for step in (1, 2, 3):
        up, down = along_y(up, 1), along_y(down, -1)
        offsets += [-step, step]
        blocks += [up, down]
    blocks.append(along_y(up, 1))
    offsets.append(-4)
    return offsets, blocks


def local(
    queries, key_vectors, value_vectors, head_kinds, block_masks, order_map, out_weight, gate_values
):
    rows, width = queries.shape
    frames = lax.axis_size("seq")
    parts = lax.axis_size("mlp")
    group = rows // frames
    masks = block_masks.reshape(-1)
    order = order_map.reshape(1, rows)
    offsets, blocks = gather_weight(out_weight)
    sent = call(
        send_kernel, (frames, group, 3 * width), [VMEM] * 4, order, queries, key_vectors, value_vectors
    )
    moved = lax.all_to_all(sent, "seq", split_axis=0, concat_axis=0, tiled=True)
    near = call(near_kernel, (rows, width), [SMEM] + [VMEM] * 3, masks, queries, key_vectors, value_vectors)
    far = call(far_kernel, (frames, group, width), [SMEM, VMEM], masks, moved)
    returned = lax.all_to_all(far, "seq", split_axis=0, concat_axis=0, tiled=True)
    attended = call(
        select_kernel, (parts, rows, width), [SMEM] + [VMEM] * 3, head_kinds, order, returned, near
    )
    columns = lax.all_to_all(attended, "mlp", split_axis=0, concat_axis=0, tiled=True)
    return call(
        functools.partial(project_kernel, offsets),
        (rows, width),
        [VMEM] * 10,
        gate_values.reshape(1, width),
        columns,
        *blocks,
    )


def solution(mesh):
    in_specs = (
        P("seq", "mlp"),
        P("seq", "mlp"),
        P("seq", "mlp"),
        P("mlp"),
        P("mlp", None, None),
        P(),
        P("seq", "mlp"),
        P("mlp"),
    )
    out_specs = P("seq", "mlp")
    return jax.shard_map(local, mesh=mesh, in_specs=in_specs, out_specs=out_specs, check_vma=False)
```

```python
import math

import jax
import jax.numpy as jnp
from jax import lax
from jax.experimental import pallas as pl
from jax.experimental.pallas import tpu as pltpu
from jax.sharding import PartitionSpec as P

HBM = pl.BlockSpec(memory_space=pltpu.HBM)
VMEM = pl.BlockSpec(memory_space=pltpu.VMEM)
LANES = 128
COST = 20 * 10**9
SMEM = pl.BlockSpec(memory_space=pltpu.SMEM)


def placement(order, rows):
    positions = lax.broadcasted_iota(jnp.int32, (rows, rows), 0)
    return (positions == order).astype(jnp.float32).astype(jnp.bfloat16)


def ones_where(condition):
    return condition.astype(jnp.float32).astype(jnp.bfloat16)


def iotas(shape):
    return lax.broadcasted_iota(jnp.int32, shape, 0), lax.broadcasted_iota(jnp.int32, shape, 1)


def send_kernel(order_hbm, q_hbm, k_hbm, v_hbm, out_ref, order_ref, x_ref, sems):
    pairs = [(order_hbm, order_ref)]
    pairs += [(src, x_ref.at[i]) for i, src in enumerate((q_hbm, k_hbm, v_hbm))]
    copies = [pltpu.make_async_copy(src, dst, sems.at[i]) for i, (src, dst) in enumerate(pairs)]
    for copy in copies:
        copy.start()
    rows, width = x_ref.shape[1:]
    copies[0].wait()
    onehot = placement(order_ref[...], rows)
    for i in range(3):
        copies[1 + i].wait()
        picked = lax.dot_general(
            onehot, x_ref[i], (((0,), (0,)), ((), ())), preferred_element_type=jnp.float32
        )
        out_ref[:, :, i * width : (i + 1) * width] = picked.reshape(
            out_ref.shape[0], out_ref.shape[1], width
        ).astype(jnp.bfloat16)


def attend(q, k, v, masks, head, row_block, column_block):
    depth = q.shape[1]
    scores = lax.dot_general(q, k, (((1,), (1,)), ((), ())), preferred_element_type=jnp.float32)
    scores = scores * (1.0 / math.sqrt(depth))
    seen = [masks[4 * head + i] for i in range(4)]
    chosen = jnp.where(
        row_block == 0,
        jnp.where(column_block == 0, seen[0], seen[1]),
        jnp.where(column_block == 0, seen[2], seen[3]),
    )
    visible = chosen == 1
    scores = jnp.where(visible, scores, -jnp.inf)
    row_max = jnp.max(scores, axis=1, keepdims=True)
    weights = jnp.exp(scores - row_max)
    total = jnp.sum(weights, axis=1, keepdims=True)
    combined = jnp.dot(weights.astype(jnp.bfloat16), v, preferred_element_type=jnp.float32)
    return combined / total


def near_kernel(masks_ref, q_ref, k_ref, v_ref, out_ref):
    rows, width = q_ref.shape
    heads = masks_ref.shape[0] // 4
    depth = width // heads
    row_block = lax.broadcasted_iota(jnp.int32, (rows, rows), 0) // (rows // 2)
    column_block = lax.broadcasted_iota(jnp.int32, (rows, rows), 1) // (rows // 2)
    for h in range(heads):
        c = slice(h * depth, (h + 1) * depth)
        out_ref[:, c] = attend(
            q_ref[:, c], k_ref[:, c], v_ref[:, c], masks_ref, h, row_block, column_block
        ).astype(jnp.bfloat16)


def message_kernel(w_ref, out_ref):
    place, row = iotas((64, w_ref.shape[0]))
    pick = ones_where((place % 16 >= 4) & (row == 12 * (place // 16) + place % 16 - 4))
    got = jnp.dot(pick, w_ref[...], preferred_element_type=jnp.float32)
    out_ref[...] = got.reshape(out_ref.shape).astype(jnp.bfloat16)


def far_kernel(masks_ref, x_ref, weights_ref, after_hbm, out_ref):
    frames, group, wide = x_ref.shape
    rows, width = frames * group, wide // 3
    heads = masks_ref.shape[0] // 4
    row, column = iotas((rows, rows))
    row_block, column_block = row % group // (group // 2), column % group // (group // 2)
    at, row = iotas((8 * frames, rows))
    spread = ones_where((at % 8 < group) & (at // 8 * group + at % 8 == row))
    for h in range(heads):
        q, k, v = (
            x_ref[:, :, i * width + h * LANES : i * width + (h + 1) * LANES]
            .astype(jnp.float32)
            .reshape(rows, LANES)
            .astype(jnp.bfloat16)
            for i in range(3)
        )
        out = attend(q, k, v, masks_ref, h, row_block, column_block).astype(jnp.bfloat16)
        out = jnp.dot(spread, out, preferred_element_type=jnp.float32)
        c = slice(h * LANES, (h + 1) * LANES)
        weights = weights_ref[:, :, c].astype(jnp.float32).reshape(1, 2, 1, 2, 16, LANES)
        first = out.reshape(4, 2, 4, 2, 8, LANES) + weights[:, :, :, :, :8]
        rest = jnp.broadcast_to(weights[:, :, :, :, 8:], first.shape)
        out_ref[:, :8, c] = first.reshape(frames, 8, LANES).astype(jnp.bfloat16)
        out_ref[:, 8:, c] = rest.reshape(frames, 8, LANES).astype(jnp.bfloat16)


def part_kernel(x_ref, after_hbm, out_ref):
    n, part, width = out_ref.shape
    row, at = iotas((part, 16 * n))
    take = ones_where(row // 12 * 16 + 4 + row % 12 == at)
    for y in range(n):
        block = x_ref[y * n : (y + 1) * n].astype(jnp.float32).reshape(16 * n, width)
        got = jnp.dot(take, block.astype(jnp.bfloat16), preferred_element_type=jnp.float32)
        out_ref[y] = got.astype(jnp.bfloat16)


def select_kernel(kinds_ref, order_ref, far_ref, near_ref, out_ref):
    rows, width = near_ref.shape
    frames = far_ref.shape[0]
    heads = kinds_ref.shape[0]
    row, at = iotas((rows, 8 * frames))
    take = ones_where(row // 4 * 8 + row % 4 == at)
    far = far_ref[:, :8, :].astype(jnp.float32).reshape(8 * frames, width).astype(jnp.bfloat16)
    far = jnp.dot(take, far, preferred_element_type=jnp.float32).astype(jnp.bfloat16)
    back = jnp.dot(placement(order_ref[...], rows), far, preferred_element_type=jnp.float32)
    place = lax.broadcasted_iota(jnp.int32, (1, width), 1)
    quarter = sum((place >= edge).astype(jnp.int32) for edge in (96, 192, 288))
    left = place - 96 * quarter
    z = sum((left >= 12 * i).astype(jnp.int32) for i in range(1, 8))
    column = 48 * z + 12 * quarter + left - 12 * z
    total = None
    for h in range(heads):
        c = slice(h * LANES, (h + 1) * LANES)
        near = near_ref[:, c].astype(jnp.float32)
        chosen = jnp.where(kinds_ref[h] == 1, back[:, c], near).astype(jnp.bfloat16)
        old = lax.broadcasted_iota(jnp.int32, (LANES, width), 0) + h * LANES
        moved = jnp.dot(chosen, ones_where(old == column), preferred_element_type=jnp.float32)
        total = moved if total is None else total + moved
    total = total.astype(jnp.bfloat16)
    for m in range(out_ref.shape[0]):
        out_ref[m] = total


def weight_kernel(own_ref, z_ref, y_ref, both_ref, out_ref):
    seq = lax.axis_index("seq")
    y, z = lax.rem(seq // 8, 2), lax.rem(seq, 2)
    part = own_ref.shape[1]
    for at_y, at_z, ref in (
        (y, z, own_ref),
        (y, 1 - z, z_ref),
        (1 - y, z, y_ref),
        (1 - y, 1 - z, both_ref),
    ):
        rows = pl.ds(pl.multiple_of((2 * at_y + at_z) * part, part), part)
        out_ref[:, rows, :] = ref[...]


def project_kernel(gate_ref, x_ref, others_ref, w_ref, out_ref):
    core = lax.rem(lax.axis_index("mlp"), 2)
    total = None
    for ref, parity in ((x_ref, core), (others_ref, 1 - core)):
        for x in range(x_ref.shape[0]):
            got = jnp.dot(ref[x], w_ref[2 * x + parity], preferred_element_type=jnp.float32)
            total = got if total is None else total + got
    out_ref[...] = (gate_ref[...] * total).astype(jnp.bfloat16)


def call(kernel, shape, specs, *args, scratch=(), limit=16, dtype=jnp.bfloat16, cost=None):
    return pl.pallas_call(
        kernel,
        out_shape=jax.ShapeDtypeStruct(shape, dtype),
        in_specs=specs,
        out_specs=VMEM,
        scratch_shapes=scratch,
        compiler_params=pltpu.CompilerParams(vmem_limit_bytes=limit * 1024 * 1024),
        cost_estimate=cost,
    )(*args)


def fetch(block, dy, dz):
    pairs = [
        ((y + dy) % 8 * 8 + (z + dz) % 8, 8 * y + z) for y in range(8) for z in range(8)
    ]
    return lax.ppermute(block, "seq", pairs)


def local(
    queries, key_vectors, value_vectors, head_kinds, block_masks, order_map, out_weight, gate_values
):
    rows, width = queries.shape
    frames = lax.axis_size("seq")
    parts = lax.axis_size("mlp")
    group = rows // frames
    masks = block_masks.reshape(-1)
    order = order_map.reshape(1, rows)
    sent = call(
        send_kernel,
        (frames, group, 3 * width),
        [HBM] * 4,
        order,
        queries,
        key_vectors,
        value_vectors,
        scratch=[
            pltpu.VMEM((1, rows), jnp.int32),
            pltpu.VMEM((3, rows, width), jnp.bfloat16),
            pltpu.SemaphoreType.DMA((4,)),
        ],
        limit=60,
    )
    moved = lax.all_to_all(sent, "seq", split_axis=0, concat_axis=0, tiled=True)
    near = call(near_kernel, (rows, width), [SMEM] + [VMEM] * 3, masks, queries, key_vectors, value_vectors)
    pieces = call(message_kernel, (4, 16, width), [VMEM], out_weight)
    far = call(
        far_kernel, (frames, 16, width), [SMEM, VMEM, VMEM, HBM], masks, moved, pieces, near
    )
    returned = lax.all_to_all(far, "seq", split_axis=0, concat_axis=0, tiled=True)

    attended = call(
        select_kernel,
        (parts // 2, rows, width),
        [SMEM] + [VMEM] * 3,
        head_kinds,
        order,
        returned,
        near,
    )
    own = call(part_kernel, (parts, 96, width), [VMEM, HBM], returned, attended)
    others = [fetch(own, dy, dz) for dy, dz in ((0, 1), (1, 0), (-1, -1))]
    columns = lax.all_to_all(
        attended,
        "mlp",
        split_axis=0,
        concat_axis=0,
        axis_index_groups=[[0, 2, 4, 6], [1, 3, 5, 7]],
        tiled=True,
    )
    others_columns = lax.ppermute(columns, "mlp", [(i, i ^ 1) for i in range(parts)])
    weight = call(
        weight_kernel,
        (parts, width, width),
        [VMEM] * 4,
        own,
        *others,
        cost=pl.CostEstimate(flops=COST, bytes_accessed=0, transcendentals=0),
    )
    return call(
        project_kernel,
        (rows, width),
        [VMEM] * 4,
        gate_values.reshape(1, width),
        columns,
        others_columns,
        weight,
    )


def solution(mesh):
    in_specs = (
        P("seq", "mlp"),
        P("seq", "mlp"),
        P("seq", "mlp"),
        P("mlp"),
        P("mlp", None, None),
        P(),
        P("seq", "mlp"),
        P("mlp"),
    )
    out_specs = P("seq", "mlp")
    return jax.shard_map(local, mesh=mesh, in_specs=in_specs, out_specs=out_specs, check_vma=False)
```

```python
import math

import jax
import jax.numpy as jnp
from jax import lax
from jax.experimental import pallas as pl
from jax.experimental.pallas import tpu as pltpu
from jax.sharding import PartitionSpec as P

HBM = pl.BlockSpec(memory_space=pltpu.HBM)
VMEM = pl.BlockSpec(memory_space=pltpu.VMEM)
LANES = 128
COST = 20 * 10**9
SMEM = pl.BlockSpec(memory_space=pltpu.SMEM)


def placement(order, rows):
    positions = lax.broadcasted_iota(jnp.int32, (rows, rows), 0)
    return (positions == order).astype(jnp.float32).astype(jnp.bfloat16)


def ones_where(condition):
    return condition.astype(jnp.float32).astype(jnp.bfloat16)


def iotas(shape):
    return lax.broadcasted_iota(jnp.int32, shape, 0), lax.broadcasted_iota(jnp.int32, shape, 1)


def send_kernel(order_hbm, q_hbm, k_hbm, v_hbm, out_ref, order_ref, x_ref, sems):
    pairs = [(order_hbm, order_ref)]
    pairs += [(src, x_ref.at[i]) for i, src in enumerate((q_hbm, k_hbm, v_hbm))]
    copies = [pltpu.make_async_copy(src, dst, sems.at[i]) for i, (src, dst) in enumerate(pairs)]
    for copy in copies:
        copy.start()
    rows, width = x_ref.shape[1:]
    copies[0].wait()
    onehot = placement(order_ref[...], rows)
    for i in range(3):
        copies[1 + i].wait()
        picked = lax.dot_general(
            onehot, x_ref[i], (((0,), (0,)), ((), ())), preferred_element_type=jnp.float32
        )
        out_ref[:, :, i * width : (i + 1) * width] = picked.reshape(
            out_ref.shape[0], out_ref.shape[1], width
        ).astype(jnp.bfloat16)


def attend(q, k, v, masks, head, row_block, column_block):
    depth = q.shape[1]
    scores = lax.dot_general(q, k, (((1,), (1,)), ((), ())), preferred_element_type=jnp.float32)
    scores = scores * (1.0 / math.sqrt(depth))
    seen = [masks[4 * head + i] for i in range(4)]
    chosen = jnp.where(
        row_block == 0,
        jnp.where(column_block == 0, seen[0], seen[1]),
        jnp.where(column_block == 0, seen[2], seen[3]),
    )
    visible = chosen == 1
    scores = jnp.where(visible, scores, -jnp.inf)
    row_max = jnp.max(scores, axis=1, keepdims=True)
    weights = jnp.exp(scores - row_max)
    total = jnp.sum(weights, axis=1, keepdims=True)
    combined = jnp.dot(weights.astype(jnp.bfloat16), v, preferred_element_type=jnp.float32)
    return combined / total


def near_kernel(masks_ref, q_ref, k_ref, v_ref, out_ref):
    rows, width = q_ref.shape
    heads = masks_ref.shape[0] // 4
    depth = width // heads
    row_block = lax.broadcasted_iota(jnp.int32, (rows, rows), 0) // (rows // 2)
    column_block = lax.broadcasted_iota(jnp.int32, (rows, rows), 1) // (rows // 2)
    for h in range(heads):
        c = slice(h * depth, (h + 1) * depth)
        out_ref[:, c] = attend(
            q_ref[:, c], k_ref[:, c], v_ref[:, c], masks_ref, h, row_block, column_block
        ).astype(jnp.bfloat16)


def quarter_of(core, y, z):
    return jnp.where(core == 0, z + 2 * y, 2 * z + y) % 4


def message_kernel(w_ref, out_ref):
    core = lax.rem(lax.axis_index("mlp"), 2)
    place, row = iotas((256, w_ref.shape[0]))
    first = 12 * quarter_of(core, place // 64, place // 16 % 4)
    pick = ones_where((place % 16 >= 4) & (row == first + place % 16 - 4))
    got = jnp.dot(pick, w_ref[...], preferred_element_type=jnp.float32)
    out_ref[...] = got.reshape(out_ref.shape).astype(jnp.bfloat16)


def far_kernel(masks_ref, x_ref, weights_ref, after_hbm, out_ref):
    frames, group, wide = x_ref.shape
    rows, width = frames * group, wide // 3
    heads = masks_ref.shape[0] // 4
    row, column = iotas((rows, rows))
    row_block, column_block = row % group // (group // 2), column % group // (group // 2)
    at, row = iotas((8 * frames, rows))
    spread = ones_where((at % 8 < group) & (at // 8 * group + at % 8 == row))
    for h in range(heads):
        q, k, v = (
            x_ref[:, :, i * width + h * LANES : i * width + (h + 1) * LANES]
            .astype(jnp.float32)
            .reshape(rows, LANES)
            .astype(jnp.bfloat16)
            for i in range(3)
        )
        out = attend(q, k, v, masks_ref, h, row_block, column_block).astype(jnp.bfloat16)
        out = jnp.dot(spread, out, preferred_element_type=jnp.float32)
        c = slice(h * LANES, (h + 1) * LANES)
        weights = weights_ref[:, :, c].astype(jnp.float32).reshape(1, 4, 1, 4, 16, LANES)
        first = out.reshape(2, 4, 2, 4, 8, LANES) + weights[:, :, :, :, :8]
        rest = jnp.broadcast_to(weights[:, :, :, :, 8:], first.shape)
        out_ref[:, :8, c] = first.reshape(frames, 8, LANES).astype(jnp.bfloat16)
        out_ref[:, 8:, c] = rest.reshape(frames, 8, LANES).astype(jnp.bfloat16)


def part_kernel(x_ref, after_hbm, out_ref):
    n, part, width = out_ref.shape
    row, at = iotas((part, 16 * n))
    take = ones_where(row // 12 * 16 + 4 + row % 12 == at)
    for y in range(n):
        block = x_ref[y * n : (y + 1) * n].astype(jnp.float32).reshape(16 * n, width)
        got = jnp.dot(take, block.astype(jnp.bfloat16), preferred_element_type=jnp.float32)
        out_ref[y] = got.astype(jnp.bfloat16)


def select_kernel(kinds_ref, order_ref, far_ref, near_ref, out_ref):
    rows, width = near_ref.shape
    heads = kinds_ref.shape[0]
    onehot = placement(order_ref[...], rows)
    place = lax.broadcasted_iota(jnp.int32, (1, width), 1)
    quarter = sum((place >= edge).astype(jnp.int32) for edge in (96, 192, 288))
    left = place - 96 * quarter
    z = sum((left >= 12 * i).astype(jnp.int32) for i in range(1, 8))
    column = 48 * z + 12 * quarter + left - 12 * z
    total = None
    for h in range(heads):
        c = slice(h * LANES, (h + 1) * LANES)
        far = far_ref[:, :8, c].astype(jnp.float32)[:, :4].reshape(rows, LANES)
        back = jnp.dot(onehot, far.astype(jnp.bfloat16), preferred_element_type=jnp.float32)
        near = near_ref[:, c].astype(jnp.float32)
        chosen = jnp.where(kinds_ref[h] == 1, back, near).astype(jnp.bfloat16)
        old = lax.broadcasted_iota(jnp.int32, (LANES, width), 0) + h * LANES
        moved = jnp.dot(chosen, ones_where(old == column), preferred_element_type=jnp.float32)
        total = moved if total is None else total + moved
    total = total.astype(jnp.bfloat16)
    for m in range(out_ref.shape[0]):
        out_ref[m] = total


def weight_kernel(own_ref, next_ref, last_ref, second_ref, out_ref):
    seq = lax.axis_index("seq")
    quarter = quarter_of(lax.rem(lax.axis_index("mlp"), 2), seq // 8, lax.rem(seq, 8))
    part = own_ref.shape[1]
    for step, ref in ((0, own_ref), (1, next_ref), (3, last_ref), (2, second_ref)):
        rows = pl.ds(pl.multiple_of(lax.rem(quarter + step, 4) * part, part), part)
        out_ref[:, rows, :] = ref[...]


def project_kernel(gate_ref, x_ref, others_ref, w_ref, out_ref):
    core = lax.rem(lax.axis_index("mlp"), 2)
    total = None
    for ref, parity in ((x_ref, core), (others_ref, 1 - core)):
        for x in range(0, x_ref.shape[0], 2):
            heads = jnp.concatenate([ref[x], ref[x + 1]], axis=1)
            weight = jnp.concatenate([w_ref[2 * x + parity], w_ref[2 * x + 2 + parity]], axis=0)
            got = jnp.dot(heads, weight, preferred_element_type=jnp.float32)
            total = got if total is None else total + got
    out_ref[...] = (gate_ref[...] * total).astype(jnp.bfloat16)


def call(kernel, shape, specs, *args, scratch=(), limit=16, dtype=jnp.bfloat16, cost=None):
    return pl.pallas_call(
        kernel,
        out_shape=jax.ShapeDtypeStruct(shape, dtype),
        in_specs=specs,
        out_specs=VMEM,
        scratch_shapes=scratch,
        compiler_params=pltpu.CompilerParams(vmem_limit_bytes=limit * 1024 * 1024),
        cost_estimate=cost,
    )(*args)


def fetch(block, offsets):
    pairs = []
    for y in range(8):
        for z in range(8):
            for m in range(8):
                dy, dz = offsets[m % 2]
                source = (y + dy) % 8 * 8 + (z + dz) % 8
                pairs.append((8 * source + m, 8 * (8 * y + z) + m))
    return lax.ppermute(block, ("seq", "mlp"), pairs)


def local(
    queries, key_vectors, value_vectors, head_kinds, block_masks, order_map, out_weight, gate_values
):
    rows, width = queries.shape
    frames = lax.axis_size("seq")
    parts = lax.axis_size("mlp")
    group = rows // frames
    masks = block_masks.reshape(-1)
    order = order_map.reshape(1, rows)
    sent = call(
        send_kernel,
        (frames, group, 3 * width),
        [HBM] * 4,
        order,
        queries,
        key_vectors,
        value_vectors,
        scratch=[
            pltpu.VMEM((1, rows), jnp.int32),
            pltpu.VMEM((3, rows, width), jnp.bfloat16),
            pltpu.SemaphoreType.DMA((4,)),
        ],
        limit=60,
    )
    moved = lax.all_to_all(sent, "seq", split_axis=0, concat_axis=0, tiled=True)
    near = call(near_kernel, (rows, width), [SMEM] + [VMEM] * 3, masks, queries, key_vectors, value_vectors)
    pieces = call(message_kernel, (16, 16, width), [VMEM], out_weight)
    far = call(
        far_kernel, (frames, 16, width), [SMEM, VMEM, VMEM, HBM], masks, moved, pieces, near
    )
    returned = lax.all_to_all(far, "seq", split_axis=0, concat_axis=0, tiled=True)

    attended = call(
        select_kernel,
        (parts // 2, rows, width),
        [SMEM] + [VMEM] * 3,
        head_kinds,
        order,
        returned,
        near,
    )
    own = call(part_kernel, (parts, 96, width), [VMEM, HBM], returned, attended)
    others = [
        fetch(own, offsets) for offsets in (((0, 1), (1, 0)), ((0, -1), (-1, 0)), ((1, 0), (0, 1)))
    ]
    columns = lax.all_to_all(
        attended,
        "mlp",
        split_axis=0,
        concat_axis=0,
        axis_index_groups=[[0, 2, 4, 6], [1, 3, 5, 7]],
        tiled=True,
    )
    others_columns = lax.ppermute(columns, "mlp", [(i, i ^ 1) for i in range(parts)])
    weight = call(
        weight_kernel,
        (parts, width, width),
        [VMEM] * 4,
        own,
        *others,
        cost=pl.CostEstimate(flops=COST, bytes_accessed=0, transcendentals=0),
    )
    return call(
        project_kernel,
        (rows, width),
        [VMEM] * 4,
        gate_values.reshape(1, width),
        columns,
        others_columns,
        weight,
    )


def solution(mesh):
    in_specs = (
        P("seq", "mlp"),
        P("seq", "mlp"),
        P("seq", "mlp"),
        P("mlp"),
        P("mlp", None, None),
        P(),
        P("seq", "mlp"),
        P("mlp"),
    )
    out_specs = P("seq", "mlp")
    return jax.shard_map(local, mesh=mesh, in_specs=in_specs, out_specs=out_specs, check_vma=False)
```

```python
import math

import jax
import jax.numpy as jnp
from jax import lax
from jax.experimental import pallas as pl
from jax.experimental.pallas import tpu as pltpu
from jax.sharding import PartitionSpec as P

HBM = pl.BlockSpec(memory_space=pltpu.HBM)
VMEM = pl.BlockSpec(memory_space=pltpu.VMEM)
LANES = 128
COST = 20 * 10**9
SMEM = pl.BlockSpec(memory_space=pltpu.SMEM)


def placement(order, rows):
    positions = lax.broadcasted_iota(jnp.int32, (rows, rows), 0)
    return (positions == order).astype(jnp.float32).astype(jnp.bfloat16)


def ones_where(condition):
    return condition.astype(jnp.float32).astype(jnp.bfloat16)


def iotas(shape):
    return lax.broadcasted_iota(jnp.int32, shape, 0), lax.broadcasted_iota(jnp.int32, shape, 1)


def send_kernel(
    order_hbm, q_hbm, k_hbm, v_hbm, out_hbm, order_ref, x_ref, out_ref, sems, out_sems
):
    pairs = [(order_hbm, order_ref)]
    pairs += [(src, x_ref.at[i]) for i, src in enumerate((q_hbm, k_hbm, v_hbm))]
    copies = [pltpu.make_async_copy(src, dst, sems.at[i]) for i, (src, dst) in enumerate(pairs)]
    for copy in copies:
        copy.start()
    rows, width = x_ref.shape[1:]
    copies[0].wait()
    onehot = placement(order_ref[...], rows)
    outs = []
    for i in range(3):
        c = slice(i * width, (i + 1) * width)
        copies[1 + i].wait()
        picked = lax.dot_general(
            onehot, x_ref[i], (((0,), (0,)), ((), ())), preferred_element_type=jnp.float32
        )
        out_ref[:, :, c] = picked.reshape(out_ref.shape[0], out_ref.shape[1], width).astype(
            jnp.bfloat16
        )
        outs.append(
            pltpu.make_async_copy(out_ref.at[:, :, c], out_hbm.at[:, :, c], out_sems.at[i])
        )
        outs[-1].start()
    for copy in outs:
        copy.wait()


def attend(q, k, v, masks, head, row_block, column_block):
    depth = q.shape[1]
    scores = lax.dot_general(q, k, (((1,), (1,)), ((), ())), preferred_element_type=jnp.float32)
    scores = scores * (1.0 / math.sqrt(depth))
    seen = [masks[4 * head + i] for i in range(4)]
    chosen = jnp.where(
        row_block == 0,
        jnp.where(column_block == 0, seen[0], seen[1]),
        jnp.where(column_block == 0, seen[2], seen[3]),
    )
    visible = chosen == 1
    scores = jnp.where(visible, scores, -jnp.inf)
    row_max = jnp.max(scores, axis=1, keepdims=True)
    weights = jnp.exp(scores - row_max)
    total = jnp.sum(weights, axis=1, keepdims=True)
    combined = jnp.dot(weights.astype(jnp.bfloat16), v, preferred_element_type=jnp.float32)
    return combined / total


def near_kernel(masks_ref, q_ref, k_ref, v_ref, out_ref):
    rows, width = q_ref.shape
    heads = masks_ref.shape[0] // 4
    depth = width // heads
    row_block = lax.broadcasted_iota(jnp.int32, (rows, rows), 0) // (rows // 2)
    column_block = lax.broadcasted_iota(jnp.int32, (rows, rows), 1) // (rows // 2)
    for h in range(heads):
        c = slice(h * depth, (h + 1) * depth)
        out_ref[:, c] = attend(
            q_ref[:, c], k_ref[:, c], v_ref[:, c], masks_ref, h, row_block, column_block
        ).astype(jnp.bfloat16)


def quarter_of(core, y, z):
    return jnp.where(core == 0, z + 2 * y, 2 * z + y) % 4


def message_kernel(w_ref, out_ref):
    core = lax.rem(lax.axis_index("mlp"), 2)
    place, row = iotas((256, w_ref.shape[0]))
    first = 12 * quarter_of(core, place // 64, place // 16 % 4)
    pick = ones_where((place % 16 >= 4) & (row == first + place % 16 - 4))
    got = jnp.dot(pick, w_ref[...], preferred_element_type=jnp.float32)
    out_ref[...] = got.reshape(out_ref.shape).astype(jnp.bfloat16)


def far_kernel(masks_ref, x_ref, weights_ref, after_hbm, out_ref):
    frames, group, wide = x_ref.shape
    rows, width = frames * group, wide // 3
    heads = masks_ref.shape[0] // 4
    row, column = iotas((rows, rows))
    row_block, column_block = row % group // (group // 2), column % group // (group // 2)
    at, row = iotas((8 * frames, rows))
    spread = ones_where((at % 8 < group) & (at // 8 * group + at % 8 == row))
    for h in range(heads):
        q, k, v = (
            x_ref[:, :, i * width + h * LANES : i * width + (h + 1) * LANES]
            .astype(jnp.float32)
            .reshape(rows, LANES)
            .astype(jnp.bfloat16)
            for i in range(3)
        )
        out = attend(q, k, v, masks_ref, h, row_block, column_block).astype(jnp.bfloat16)
        out = jnp.dot(spread, out, preferred_element_type=jnp.float32)
        c = slice(h * LANES, (h + 1) * LANES)
        weights = weights_ref[:, :, c].reshape(1, 4, 1, 4, 16, LANES)
        first = out.reshape(2, 4, 2, 4, 8, LANES) + weights[:, :, :, :, :8].astype(jnp.float32)
        rest = jnp.broadcast_to(weights[:, :, :, :, 8:], first.shape)
        out_ref[:, :8, c] = first.reshape(frames, 8, LANES).astype(jnp.bfloat16)
        out_ref[:, 8:, c] = rest.reshape(frames, 8, LANES)


def select_kernel(
    kinds_ref, order_ref, far_ref, near_ref, out_hbm, own_ref, out_ref, sems
):
    rows, width = near_ref.shape
    heads = kinds_ref.shape[0]
    onehot = placement(order_ref[...], rows)
    place = lax.broadcasted_iota(jnp.int32, (1, width), 1)
    quarter = sum((place >= edge).astype(jnp.int32) for edge in (96, 192, 288))
    left = place - 96 * quarter
    z = sum((left >= 12 * i).astype(jnp.int32) for i in range(1, 8))
    column = 48 * z + 12 * quarter + left - 12 * z
    total = None
    for h in range(heads):
        c = slice(h * LANES, (h + 1) * LANES)
        far = far_ref[:, :8, c].astype(jnp.float32)[:, :4].reshape(rows, LANES)
        back = jnp.dot(onehot, far.astype(jnp.bfloat16), preferred_element_type=jnp.float32)
        near = near_ref[:, c].astype(jnp.float32)
        chosen = jnp.where(kinds_ref[h] == 1, back, near).astype(jnp.bfloat16)
        old = lax.broadcasted_iota(jnp.int32, (LANES, width), 0) + h * LANES
        moved = jnp.dot(chosen, ones_where(old == column), preferred_element_type=jnp.float32)
        total = moved if total is None else total + moved
    out_ref[...] = total.astype(jnp.bfloat16)
    copies = [
        pltpu.make_async_copy(out_ref, out_hbm.at[x], sems.at[x]) for x in range(out_hbm.shape[0])
    ]
    for copy in copies:
        copy.start()
    n, part = own_ref.shape[:2]
    row, at = iotas((part, 16 * n))
    take = ones_where(row // 12 * 16 + 4 + row % 12 == at)
    for y in range(n):
        block = far_ref[y * n : (y + 1) * n].astype(jnp.float32).reshape(16 * n, width)
        got = jnp.dot(take, block.astype(jnp.bfloat16), preferred_element_type=jnp.float32)
        own_ref[y] = got.astype(jnp.bfloat16)
    for copy in copies:
        copy.wait()


def weight_kernel(own_ref, next_ref, last_ref, second_ref, out_ref):
    seq = lax.axis_index("seq")
    quarter = quarter_of(lax.rem(lax.axis_index("mlp"), 2), seq // 8, lax.rem(seq, 8))
    part = own_ref.shape[1]
    for step, ref in ((0, own_ref), (1, next_ref), (3, last_ref), (2, second_ref)):
        rows = pl.ds(pl.multiple_of(lax.rem(quarter + step, 4) * part, part), part)
        out_ref[:, rows, :] = ref[...]


def project_kernel(gate_ref, x_ref, others_ref, w_ref, out_ref):
    core = lax.rem(lax.axis_index("mlp"), 2)
    total = None
    for ref, parity in ((x_ref, core), (others_ref, 1 - core)):
        for x in range(0, x_ref.shape[0], 2):
            heads = jnp.concatenate([ref[x], ref[x + 1]], axis=1)
            weight = jnp.concatenate([w_ref[2 * x + parity], w_ref[2 * x + 2 + parity]], axis=0)
            got = jnp.dot(heads, weight, preferred_element_type=jnp.float32)
            total = got if total is None else total + got
    out_ref[...] = (gate_ref[...] * total).astype(jnp.bfloat16)


def call(kernel, shape, specs, *args, out=VMEM, scratch=(), limit=16, cost=None):
    shapes = shape if isinstance(shape, list) else [shape]
    shapes = [jax.ShapeDtypeStruct(one, jnp.bfloat16) for one in shapes]
    return pl.pallas_call(
        kernel,
        out_shape=shapes if isinstance(shape, list) else shapes[0],
        in_specs=specs,
        out_specs=out,
        scratch_shapes=scratch,
        compiler_params=pltpu.CompilerParams(vmem_limit_bytes=limit * 1024 * 1024),
        cost_estimate=cost,
    )(*args)


def fetch(block, offsets):
    pairs = []
    for y in range(8):
        for z in range(8):
            for m in range(8):
                dy, dz = offsets[m % 2]
                source = (y + dy) % 8 * 8 + (z + dz) % 8
                pairs.append((8 * source + m, 8 * (8 * y + z) + m))
    return lax.ppermute(block, ("seq", "mlp"), pairs)


def local(
    queries, key_vectors, value_vectors, head_kinds, block_masks, order_map, out_weight, gate_values
):
    rows, width = queries.shape
    frames = lax.axis_size("seq")
    parts = lax.axis_size("mlp")
    group = rows // frames
    masks = block_masks.reshape(-1)
    order = order_map.reshape(1, rows)
    sent = call(
        send_kernel,
        (frames, group, 3 * width),
        [HBM] * 4,
        order,
        queries,
        key_vectors,
        value_vectors,
        scratch=[
            pltpu.VMEM((1, rows), jnp.int32),
            pltpu.VMEM((3, rows, width), jnp.bfloat16),
            pltpu.VMEM((frames, group, 3 * width), jnp.bfloat16),
            pltpu.SemaphoreType.DMA((4,)),
            pltpu.SemaphoreType.DMA((3,)),
        ],
        out=HBM,
        limit=60,
    )
    moved = lax.all_to_all(sent, "seq", split_axis=0, concat_axis=0, tiled=True)
    near = call(near_kernel, (rows, width), [SMEM] + [VMEM] * 3, masks, queries, key_vectors, value_vectors)
    pieces = call(message_kernel, (16, 16, width), [VMEM], out_weight)
    far = call(
        far_kernel, (frames, 16, width), [SMEM, VMEM, VMEM, HBM], masks, moved, pieces, near
    )
    returned = lax.all_to_all(far, "seq", split_axis=0, concat_axis=0, tiled=True)

    attended, own = call(
        select_kernel,
        [(parts // 2, rows, width), (parts, 96, width)],
        [SMEM] + [VMEM] * 3,
        head_kinds,
        order,
        returned,
        near,
        out=[HBM, VMEM],
        scratch=[pltpu.VMEM((rows, width), jnp.bfloat16), pltpu.SemaphoreType.DMA((parts // 2,))],
    )
    others = [
        fetch(own, offsets) for offsets in (((0, 1), (1, 0)), ((0, -1), (-1, 0)), ((1, 0), (0, 1)))
    ]
    columns = lax.all_to_all(
        attended,
        "mlp",
        split_axis=0,
        concat_axis=0,
        axis_index_groups=[[0, 2, 4, 6], [1, 3, 5, 7]],
        tiled=True,
    )
    others_columns = lax.ppermute(columns, "mlp", [(i, i ^ 1) for i in range(parts)])
    weight = call(
        weight_kernel,
        (parts, width, width),
        [VMEM] * 4,
        own,
        *others,
        cost=pl.CostEstimate(flops=COST, bytes_accessed=0, transcendentals=0),
    )
    return call(
        project_kernel,
        (rows, width),
        [VMEM] * 4,
        gate_values.reshape(1, width),
        columns,
        others_columns,
        weight,
    )


def solution(mesh):
    in_specs = (
        P("seq", "mlp"),
        P("seq", "mlp"),
        P("seq", "mlp"),
        P("mlp"),
        P("mlp", None, None),
        P(),
        P("seq", "mlp"),
        P("mlp"),
    )
    out_specs = P("seq", "mlp")
    return jax.shard_map(local, mesh=mesh, in_specs=in_specs, out_specs=out_specs, check_vma=False)
```

```python
import math

import jax
import jax.numpy as jnp
from jax import lax
from jax.experimental import pallas as pl
from jax.experimental.pallas import tpu as pltpu
from jax.sharding import PartitionSpec as P

HBM = pl.BlockSpec(memory_space=pltpu.HBM)
VMEM = pl.BlockSpec(memory_space=pltpu.VMEM)
LANES = 128
COST = 20 * 10**9
SMEM = pl.BlockSpec(memory_space=pltpu.SMEM)


def placement(order, rows):
    positions = lax.broadcasted_iota(jnp.int32, (rows, rows), 0)
    return (positions == order).astype(jnp.float32).astype(jnp.bfloat16)


def ones_where(condition):
    return condition.astype(jnp.float32).astype(jnp.bfloat16)


def iotas(shape):
    return lax.broadcasted_iota(jnp.int32, shape, 0), lax.broadcasted_iota(jnp.int32, shape, 1)


def send_kernel(
    order_hbm, q_hbm, k_hbm, v_hbm, out_hbm, order_ref, x_ref, out_ref, sems, out_sems
):
    pairs = [(order_hbm, order_ref)]
    pairs += [(src, x_ref.at[i]) for i, src in enumerate((q_hbm, k_hbm, v_hbm))]
    copies = [pltpu.make_async_copy(src, dst, sems.at[i]) for i, (src, dst) in enumerate(pairs)]
    for copy in copies:
        copy.start()
    rows, width = x_ref.shape[1:]
    copies[0].wait()
    onehot = placement(order_ref[...], rows)
    outs = []
    for i in range(3):
        c = slice(i * width, (i + 1) * width)
        copies[1 + i].wait()
        picked = lax.dot_general(
            onehot, x_ref[i], (((0,), (0,)), ((), ())), preferred_element_type=jnp.float32
        )
        out_ref[:, :, c] = picked.reshape(out_ref.shape[0], out_ref.shape[1], width).astype(
            jnp.bfloat16
        )
        outs.append(
            pltpu.make_async_copy(out_ref.at[:, :, c], out_hbm.at[:, :, c], out_sems.at[i])
        )
        outs[-1].start()
    for copy in outs:
        copy.wait()


def attend(q, k, v, masks, head, row_block, column_block):
    depth = q.shape[1]
    scores = lax.dot_general(q, k, (((1,), (1,)), ((), ())), preferred_element_type=jnp.float32)
    scores = scores * (1.0 / math.sqrt(depth))
    seen = [masks[4 * head + i] for i in range(4)]
    chosen = jnp.where(
        row_block == 0,
        jnp.where(column_block == 0, seen[0], seen[1]),
        jnp.where(column_block == 0, seen[2], seen[3]),
    )
    visible = chosen == 1
    scores = jnp.where(visible, scores, -jnp.inf)
    row_max = jnp.max(scores, axis=1, keepdims=True)
    weights = jnp.exp(scores - row_max)
    total = jnp.sum(weights, axis=1, keepdims=True)
    combined = jnp.dot(weights.astype(jnp.bfloat16), v, preferred_element_type=jnp.float32)
    return combined / total


def near_kernel(masks_ref, q_ref, k_ref, v_ref, out_ref):
    rows, width = q_ref.shape
    heads = masks_ref.shape[0] // 4
    depth = width // heads
    row_block = lax.broadcasted_iota(jnp.int32, (rows, rows), 0) // (rows // 2)
    column_block = lax.broadcasted_iota(jnp.int32, (rows, rows), 1) // (rows // 2)
    for h in range(heads):
        c = slice(h * depth, (h + 1) * depth)
        out_ref[:, c] = attend(
            q_ref[:, c], k_ref[:, c], v_ref[:, c], masks_ref, h, row_block, column_block
        ).astype(jnp.bfloat16)


def quarter_of(core, y, z):
    return jnp.where(core == 0, z + 2 * y, 2 * z + y) % 4


def message_kernel(w_ref, out_ref):
    core = lax.rem(lax.axis_index("mlp"), 2)
    place, row = iotas((256, w_ref.shape[0]))
    first = 12 * quarter_of(core, place // 64, place // 16 % 4)
    pick = ones_where((place % 16 >= 4) & (row == first + place % 16 - 4))
    got = jnp.dot(pick, w_ref[...], preferred_element_type=jnp.float32)
    out_ref[...] = got.reshape(out_ref.shape).astype(jnp.bfloat16)


def far_kernel(masks_ref, x_ref, weights_ref, after_hbm, out_ref):
    frames, group, wide = x_ref.shape
    rows, width = frames * group, wide // 3
    heads = masks_ref.shape[0] // 4
    row, column = iotas((rows, rows))
    row_block, column_block = row % group // (group // 2), column % group // (group // 2)
    at, row = iotas((8 * frames, rows))
    spread = ones_where((at % 8 < group) & (at // 8 * group + at % 8 == row))
    outs = []
    for h in range(heads):
        q, k, v = (
            x_ref[:, :, i * width + h * LANES : i * width + (h + 1) * LANES]
            .astype(jnp.float32)
            .reshape(rows, LANES)
            .astype(jnp.bfloat16)
            for i in range(3)
        )
        out = attend(q, k, v, masks_ref, h, row_block, column_block)
        outs.append(out.astype(jnp.bfloat16))
    out = jnp.dot(spread, jnp.concatenate(outs, axis=1), preferred_element_type=jnp.float32)
    weights = weights_ref[...].reshape(1, 4, 1, 4, 16, width)
    first = out.reshape(2, 4, 2, 4, 8, width) + weights[:, :, :, :, :8].astype(jnp.float32)
    rest = jnp.broadcast_to(weights[:, :, :, :, 8:], first.shape)
    out_ref[:, :8, :] = first.reshape(frames, 8, width).astype(jnp.bfloat16)
    out_ref[:, 8:, :] = rest.reshape(frames, 8, width)


def select_kernel(
    kinds_ref, order_ref, far_ref, near_ref, out_hbm, own_ref, out_ref, sems
):
    rows, width = near_ref.shape
    heads = kinds_ref.shape[0]
    onehot = placement(order_ref[...], rows)
    place = lax.broadcasted_iota(jnp.int32, (1, width), 1)
    quarter = sum((place >= edge).astype(jnp.int32) for edge in (96, 192, 288))
    left = place - 96 * quarter
    z = sum((left >= 12 * i).astype(jnp.int32) for i in range(1, 8))
    column = 48 * z + 12 * quarter + left - 12 * z
    old = lax.broadcasted_iota(jnp.int32, (width, width), 0)
    to_weight = ones_where(old == column)
    far = far_ref[:, :8, :].astype(jnp.float32)[:, :4].reshape(rows, width).astype(jnp.bfloat16)
    copies = []
    for half in range(2):
        r = slice(half * rows // 2, (half + 1) * rows // 2)
        back = jnp.dot(onehot[r], far, preferred_element_type=jnp.float32)
        near = near_ref[r, :].astype(jnp.float32)
        chosen = []
        for h in range(heads):
            c = slice(h * LANES, (h + 1) * LANES)
            chosen.append(jnp.where(kinds_ref[h] == 1, back[:, c], near[:, c]).astype(jnp.bfloat16))
        moved = jnp.dot(
            jnp.concatenate(chosen, axis=1), to_weight, preferred_element_type=jnp.float32
        )
        out_ref[r, :] = moved.astype(jnp.bfloat16)
        for x in range(out_hbm.shape[0]):
            copies.append(
                pltpu.make_async_copy(out_ref.at[r], out_hbm.at[x, r], sems.at[2 * x + half])
            )
            copies[-1].start()
    n, part = own_ref.shape[:2]
    row, at = iotas((part, 16 * n))
    take = ones_where(row // 12 * 16 + 4 + row % 12 == at)
    for y in range(n):
        block = far_ref[y * n : (y + 1) * n].astype(jnp.float32).reshape(16 * n, width)
        got = jnp.dot(take, block.astype(jnp.bfloat16), preferred_element_type=jnp.float32)
        own_ref[y] = got.astype(jnp.bfloat16)
    for copy in copies:
        copy.wait()


def weight_kernel(own_ref, next_ref, last_ref, second_ref, out_ref):
    seq = lax.axis_index("seq")
    quarter = quarter_of(lax.rem(lax.axis_index("mlp"), 2), seq // 8, lax.rem(seq, 8))
    part = own_ref.shape[1]
    for step, ref in ((0, own_ref), (1, next_ref), (3, last_ref), (2, second_ref)):
        rows = pl.ds(pl.multiple_of(lax.rem(quarter + step, 4) * part, part), part)
        out_ref[:, rows, :] = ref[...]


def project_kernel(gate_ref, x_ref, others_ref, w_ref, out_ref):
    core = lax.rem(lax.axis_index("mlp"), 2)
    total = None
    for ref, parity in ((x_ref, core), (others_ref, 1 - core)):
        for x in range(0, x_ref.shape[0], 2):
            heads = jnp.concatenate([ref[x], ref[x + 1]], axis=1)
            weight = jnp.concatenate([w_ref[2 * x + parity], w_ref[2 * x + 2 + parity]], axis=0)
            got = jnp.dot(heads, weight, preferred_element_type=jnp.float32)
            total = got if total is None else total + got
    out_ref[...] = (gate_ref[...] * total).astype(jnp.bfloat16)


def call(kernel, shape, specs, *args, out=VMEM, scratch=(), limit=16, cost=None):
    shapes = shape if isinstance(shape, list) else [shape]
    shapes = [jax.ShapeDtypeStruct(one, jnp.bfloat16) for one in shapes]
    return pl.pallas_call(
        kernel,
        out_shape=shapes if isinstance(shape, list) else shapes[0],
        in_specs=specs,
        out_specs=out,
        scratch_shapes=scratch,
        compiler_params=pltpu.CompilerParams(vmem_limit_bytes=limit * 1024 * 1024),
        cost_estimate=cost,
    )(*args)


def fetch(block, offsets):
    pairs = []
    for y in range(8):
        for z in range(8):
            for m in range(8):
                dy, dz = offsets[m % 2]
                source = (y + dy) % 8 * 8 + (z + dz) % 8
                pairs.append((8 * source + m, 8 * (8 * y + z) + m))
    return lax.ppermute(block, ("seq", "mlp"), pairs)


def local(
    queries, key_vectors, value_vectors, head_kinds, block_masks, order_map, out_weight, gate_values
):
    rows, width = queries.shape
    frames = lax.axis_size("seq")
    parts = lax.axis_size("mlp")
    group = rows // frames
    masks = block_masks.reshape(-1)
    order = order_map.reshape(1, rows)
    sent = call(
        send_kernel,
        (frames, group, 3 * width),
        [HBM] * 4,
        order,
        queries,
        key_vectors,
        value_vectors,
        scratch=[
            pltpu.VMEM((1, rows), jnp.int32),
            pltpu.VMEM((3, rows, width), jnp.bfloat16),
            pltpu.VMEM((frames, group, 3 * width), jnp.bfloat16),
            pltpu.SemaphoreType.DMA((4,)),
            pltpu.SemaphoreType.DMA((3,)),
        ],
        out=HBM,
        limit=60,
    )
    moved = lax.all_to_all(sent, "seq", split_axis=0, concat_axis=0, tiled=True)
    near = call(near_kernel, (rows, width), [SMEM] + [VMEM] * 3, masks, queries, key_vectors, value_vectors)
    pieces = call(message_kernel, (16, 16, width), [VMEM], out_weight)
    far = call(
        far_kernel, (frames, 16, width), [SMEM, VMEM, VMEM, HBM], masks, moved, pieces, near
    )
    returned = lax.all_to_all(far, "seq", split_axis=0, concat_axis=0, tiled=True)

    attended, own = call(
        select_kernel,
        [(parts // 2, rows, width), (parts, 96, width)],
        [SMEM] + [VMEM] * 3,
        head_kinds,
        order,
        returned,
        near,
        out=[HBM, VMEM],
        scratch=[pltpu.VMEM((rows, width), jnp.bfloat16), pltpu.SemaphoreType.DMA((parts,))],
    )
    others = [
        fetch(own, offsets) for offsets in (((0, 1), (1, 0)), ((0, -1), (-1, 0)), ((1, 0), (0, 1)))
    ]
    columns = lax.all_to_all(
        attended,
        "mlp",
        split_axis=0,
        concat_axis=0,
        axis_index_groups=[[0, 2, 4, 6], [1, 3, 5, 7]],
        tiled=True,
    )
    others_columns = lax.ppermute(columns, "mlp", [(i, i ^ 1) for i in range(parts)])
    weight = call(
        weight_kernel,
        (parts, width, width),
        [VMEM] * 4,
        own,
        *others,
        cost=pl.CostEstimate(flops=COST, bytes_accessed=0, transcendentals=0),
    )
    return call(
        project_kernel,
        (rows, width),
        [VMEM] * 4,
        gate_values.reshape(1, width),
        columns,
        others_columns,
        weight,
    )


def solution(mesh):
    in_specs = (
        P("seq", "mlp"),
        P("seq", "mlp"),
        P("seq", "mlp"),
        P("mlp"),
        P("mlp", None, None),
        P(),
        P("seq", "mlp"),
        P("mlp"),
    )
    out_specs = P("seq", "mlp")
    return jax.shard_map(local, mesh=mesh, in_specs=in_specs, out_specs=out_specs, check_vma=False)
```

```python
import math

import jax
import jax.numpy as jnp
from jax import lax
from jax.experimental import pallas as pl
from jax.experimental.pallas import tpu as pltpu
from jax.sharding import PartitionSpec as P

HBM = pl.BlockSpec(memory_space=pltpu.HBM)
VMEM = pl.BlockSpec(memory_space=pltpu.VMEM)
LANES = 128
COST = 20 * 10**9
SMEM = pl.BlockSpec(memory_space=pltpu.SMEM)


def placement(order, rows):
    positions = lax.broadcasted_iota(jnp.int32, (rows, rows), 0)
    return (positions == order).astype(jnp.float32).astype(jnp.bfloat16)


def ones_where(condition):
    return condition.astype(jnp.float32).astype(jnp.bfloat16)


def iotas(shape):
    return lax.broadcasted_iota(jnp.int32, shape, 0), lax.broadcasted_iota(jnp.int32, shape, 1)


def send_kernel(
    order_hbm, q_hbm, k_hbm, v_hbm, out_hbm, order_ref, x_ref, out_ref, sems, out_sems
):
    pairs = [(order_hbm, order_ref)]
    pairs += [(src, x_ref.at[i]) for i, src in enumerate((q_hbm, k_hbm, v_hbm))]
    copies = [pltpu.make_async_copy(src, dst, sems.at[i]) for i, (src, dst) in enumerate(pairs)]
    for copy in copies:
        copy.start()
    rows, width = x_ref.shape[1:]
    copies[0].wait()
    onehot = placement(order_ref[...], rows)
    outs = []
    for i in range(3):
        c = slice(i * width, (i + 1) * width)
        copies[1 + i].wait()
        picked = lax.dot_general(
            onehot, x_ref[i], (((0,), (0,)), ((), ())), preferred_element_type=jnp.float32
        )
        out_ref[:, :, c] = picked.reshape(out_ref.shape[0], out_ref.shape[1], width).astype(
            jnp.bfloat16
        )
        outs.append(
            pltpu.make_async_copy(out_ref.at[:, :, c], out_hbm.at[:, :, c], out_sems.at[i])
        )
        outs[-1].start()
    for copy in outs:
        copy.wait()


def attend(q, k, v, masks, head, row_block, column_block):
    depth = q.shape[1]
    scores = lax.dot_general(q, k, (((1,), (1,)), ((), ())), preferred_element_type=jnp.float32)
    scores = scores * (1.0 / math.sqrt(depth))
    seen = [masks[4 * head + i] for i in range(4)]
    chosen = jnp.where(
        row_block == 0,
        jnp.where(column_block == 0, seen[0], seen[1]),
        jnp.where(column_block == 0, seen[2], seen[3]),
    )
    visible = chosen == 1
    scores = jnp.where(visible, scores, -jnp.inf)
    row_max = jnp.max(scores, axis=1, keepdims=True)
    weights = jnp.exp(scores - row_max)
    total = jnp.sum(weights, axis=1, keepdims=True)
    combined = jnp.dot(weights.astype(jnp.bfloat16), v, preferred_element_type=jnp.float32)
    return combined / total


def near_kernel(masks_ref, q_ref, k_ref, v_ref, out_ref):
    rows, width = q_ref.shape
    heads = masks_ref.shape[0] // 4
    depth = width // heads
    row_block = lax.broadcasted_iota(jnp.int32, (rows, rows), 0) // (rows // 2)
    column_block = lax.broadcasted_iota(jnp.int32, (rows, rows), 1) // (rows // 2)
    for h in range(heads):
        c = slice(h * depth, (h + 1) * depth)
        out_ref[:, c] = attend(
            q_ref[:, c], k_ref[:, c], v_ref[:, c], masks_ref, h, row_block, column_block
        ).astype(jnp.bfloat16)


def quarter_of(core, y, z):
    return jnp.where(core == 0, z + 2 * y, 2 * z + y) % 4


def message_kernel(w_ref, out_ref):
    core = lax.rem(lax.axis_index("mlp"), 2)
    place, row = iotas((256, w_ref.shape[0]))
    first = 12 * quarter_of(core, place // 64, place // 16 % 4)
    pick = ones_where((place % 16 >= 4) & (row == first + place % 16 - 4))
    got = jnp.dot(pick, w_ref[...], preferred_element_type=jnp.float32)
    out_ref[...] = got.reshape(out_ref.shape).astype(jnp.bfloat16)


def far_kernel(masks_ref, x_ref, weights_ref, after_hbm, out_ref):
    frames, group, wide = x_ref.shape
    rows, width = frames * group, wide // 3
    heads = masks_ref.shape[0] // 4
    row, column = iotas((rows, rows))
    row_block, column_block = row % group // (group // 2), column % group // (group // 2)
    at, row = iotas((8 * frames, rows))
    spread = ones_where((at % 8 < group) & (at // 8 * group + at % 8 == row))
    outs = []
    for h in range(heads):
        q, k, v = (
            x_ref[:, :, i * width + h * LANES : i * width + (h + 1) * LANES]
            .astype(jnp.float32)
            .reshape(rows, LANES)
            .astype(jnp.bfloat16)
            for i in range(3)
        )
        out = attend(q, k, v, masks_ref, h, row_block, column_block)
        outs.append(out.astype(jnp.bfloat16))
    out = jnp.dot(spread, jnp.concatenate(outs, axis=1), preferred_element_type=jnp.float32)
    weights = weights_ref[...].astype(jnp.float32).reshape(1, 4, 1, 4, 16, width)
    first = out.reshape(2, 4, 2, 4, 8, width) + weights[:, :, :, :, :8]
    rest = jnp.broadcast_to(weights[:, :, :, :, 8:], first.shape)
    message = jnp.concatenate(
        [first.reshape(frames, 8, width), rest.reshape(frames, 8, width)], axis=1
    )
    out_ref[...] = message.astype(jnp.bfloat16)


def select_kernel(
    kinds_ref, order_ref, far_ref, near_ref, out_hbm, own_ref, out_ref, sems
):
    rows, width = near_ref.shape
    heads = kinds_ref.shape[0]
    onehot = placement(order_ref[...], rows)
    place = lax.broadcasted_iota(jnp.int32, (1, width), 1)
    quarter = sum((place >= edge).astype(jnp.int32) for edge in (96, 192, 288))
    left = place - 96 * quarter
    z = sum((left >= 12 * i).astype(jnp.int32) for i in range(1, 8))
    column = 48 * z + 12 * quarter + left - 12 * z
    old = lax.broadcasted_iota(jnp.int32, (width, width), 0)
    to_weight = ones_where(old == column)
    far = far_ref[...].astype(jnp.float32)[:, :4].reshape(rows, width).astype(jnp.bfloat16)
    copies = []
    for half in range(2):
        r = slice(half * rows // 2, (half + 1) * rows // 2)
        back = jnp.dot(onehot[r], far, preferred_element_type=jnp.float32)
        near = near_ref[r, :].astype(jnp.float32)
        chosen = []
        for h in range(heads):
            c = slice(h * LANES, (h + 1) * LANES)
            chosen.append(jnp.where(kinds_ref[h] == 1, back[:, c], near[:, c]).astype(jnp.bfloat16))
        moved = jnp.dot(
            jnp.concatenate(chosen, axis=1), to_weight, preferred_element_type=jnp.float32
        )
        out_ref[r, :] = moved.astype(jnp.bfloat16)
        for x in range(out_hbm.shape[0]):
            copies.append(
                pltpu.make_async_copy(out_ref.at[r], out_hbm.at[x, r], sems.at[2 * x + half])
            )
            copies[-1].start()
    n, part = own_ref.shape[:2]
    row, at = iotas((part, 16 * n))
    take = ones_where(row // 12 * 16 + 4 + row % 12 == at)
    for y in range(n):
        block = far_ref[y * n : (y + 1) * n].astype(jnp.float32).reshape(16 * n, width)
        got = jnp.dot(take, block.astype(jnp.bfloat16), preferred_element_type=jnp.float32)
        own_ref[y] = got.astype(jnp.bfloat16)
    for copy in copies:
        copy.wait()


def weight_kernel(own_ref, next_ref, last_ref, second_ref, out_ref):
    seq = lax.axis_index("seq")
    quarter = quarter_of(lax.rem(lax.axis_index("mlp"), 2), seq // 8, lax.rem(seq, 8))
    part = own_ref.shape[1]
    for step, ref in ((0, own_ref), (1, next_ref), (3, last_ref), (2, second_ref)):
        rows = pl.ds(pl.multiple_of(lax.rem(quarter + step, 4) * part, part), part)
        out_ref[:, rows, :] = ref[...]


def project_kernel(gate_ref, x_ref, others_ref, w_ref, out_ref):
    core = lax.rem(lax.axis_index("mlp"), 2)
    total = None
    for ref, parity in ((x_ref, core), (others_ref, 1 - core)):
        for x in range(0, x_ref.shape[0], 2):
            heads = jnp.concatenate([ref[x], ref[x + 1]], axis=1)
            weight = jnp.concatenate([w_ref[2 * x + parity], w_ref[2 * x + 2 + parity]], axis=0)
            got = jnp.dot(heads, weight, preferred_element_type=jnp.float32)
            total = got if total is None else total + got
    out_ref[...] = (gate_ref[...] * total).astype(jnp.bfloat16)


def call(kernel, shape, specs, *args, out=VMEM, scratch=(), limit=16, cost=None):
    shapes = shape if isinstance(shape, list) else [shape]
    shapes = [jax.ShapeDtypeStruct(one, jnp.bfloat16) for one in shapes]
    return pl.pallas_call(
        kernel,
        out_shape=shapes if isinstance(shape, list) else shapes[0],
        in_specs=specs,
        out_specs=out,
        scratch_shapes=scratch,
        compiler_params=pltpu.CompilerParams(vmem_limit_bytes=limit * 1024 * 1024),
        cost_estimate=cost,
    )(*args)


def fetch(block, offsets):
    pairs = []
    for y in range(8):
        for z in range(8):
            for m in range(8):
                dy, dz = offsets[m % 2]
                source = (y + dy) % 8 * 8 + (z + dz) % 8
                pairs.append((8 * source + m, 8 * (8 * y + z) + m))
    return lax.ppermute(block, ("seq", "mlp"), pairs)


def local(
    queries, key_vectors, value_vectors, head_kinds, block_masks, order_map, out_weight, gate_values
):
    rows, width = queries.shape
    frames = lax.axis_size("seq")
    parts = lax.axis_size("mlp")
    group = rows // frames
    masks = block_masks.reshape(-1)
    order = order_map.reshape(1, rows)
    sent = call(
        send_kernel,
        (frames, group, 3 * width),
        [HBM] * 4,
        order,
        queries,
        key_vectors,
        value_vectors,
        scratch=[
            pltpu.VMEM((1, rows), jnp.int32),
            pltpu.VMEM((3, rows, width), jnp.bfloat16),
            pltpu.VMEM((frames, group, 3 * width), jnp.bfloat16),
            pltpu.SemaphoreType.DMA((4,)),
            pltpu.SemaphoreType.DMA((3,)),
        ],
        out=HBM,
        limit=60,
    )
    moved = lax.all_to_all(sent, "seq", split_axis=0, concat_axis=0, tiled=True)
    near = call(near_kernel, (rows, width), [SMEM] + [VMEM] * 3, masks, queries, key_vectors, value_vectors)
    pieces = call(message_kernel, (16, 16, width), [VMEM], out_weight)
    far = call(
        far_kernel, (frames, 16, width), [SMEM, VMEM, VMEM, HBM], masks, moved, pieces, near
    )
    returned = lax.all_to_all(far, "seq", split_axis=0, concat_axis=0, tiled=True)

    attended, own = call(
        select_kernel,
        [(parts // 2, rows, width), (parts, 96, width)],
        [SMEM] + [VMEM] * 3,
        head_kinds,
        order,
        returned,
        near,
        out=[HBM, VMEM],
        scratch=[pltpu.VMEM((rows, width), jnp.bfloat16), pltpu.SemaphoreType.DMA((parts,))],
    )
    others = [
        fetch(own, offsets) for offsets in (((0, 1), (1, 0)), ((0, -1), (-1, 0)), ((1, 0), (0, 1)))
    ]
    columns = lax.all_to_all(
        attended,
        "mlp",
        split_axis=0,
        concat_axis=0,
        axis_index_groups=[[0, 2, 4, 6], [1, 3, 5, 7]],
        tiled=True,
    )
    others_columns = lax.ppermute(columns, "mlp", [(i, i ^ 1) for i in range(parts)])
    weight = call(
        weight_kernel,
        (parts, width, width),
        [VMEM] * 4,
        own,
        *others,
        cost=pl.CostEstimate(flops=COST, bytes_accessed=0, transcendentals=0),
    )
    return call(
        project_kernel,
        (rows, width),
        [VMEM] * 4,
        gate_values.reshape(1, width),
        columns,
        others_columns,
        weight,
    )


def solution(mesh):
    in_specs = (
        P("seq", "mlp"),
        P("seq", "mlp"),
        P("seq", "mlp"),
        P("mlp"),
        P("mlp", None, None),
        P(),
        P("seq", "mlp"),
        P("mlp"),
    )
    out_specs = P("seq", "mlp")
    return jax.shard_map(local, mesh=mesh, in_specs=in_specs, out_specs=out_specs, check_vma=False)
```

```python
import math

import jax
import jax.numpy as jnp
from jax import lax
from jax.experimental import pallas as pl
from jax.experimental.pallas import tpu as pltpu
from jax.sharding import PartitionSpec as P

HBM = pl.BlockSpec(memory_space=pltpu.HBM)
VMEM = pl.BlockSpec(memory_space=pltpu.VMEM)
LANES = 128
COST = 20 * 10**9
SMEM = pl.BlockSpec(memory_space=pltpu.SMEM)


def placement(order, rows):
    positions = lax.broadcasted_iota(jnp.int32, (rows, rows), 0)
    return (positions == order).astype(jnp.float32).astype(jnp.bfloat16)


def ones_where(condition):
    return condition.astype(jnp.float32).astype(jnp.bfloat16)


def iotas(shape):
    return lax.broadcasted_iota(jnp.int32, shape, 0), lax.broadcasted_iota(jnp.int32, shape, 1)


def send_kernel(
    order_hbm, q_hbm, k_hbm, v_hbm, out_hbm, order_ref, x_ref, out_ref, sems, out_sems
):
    pairs = [(order_hbm, order_ref)]
    pairs += [(src, x_ref.at[i]) for i, src in enumerate((q_hbm, k_hbm, v_hbm))]
    copies = [pltpu.make_async_copy(src, dst, sems.at[i]) for i, (src, dst) in enumerate(pairs)]
    for copy in copies:
        copy.start()
    rows, width = x_ref.shape[1:]
    copies[0].wait()
    onehot = placement(order_ref[...], rows)
    outs = []
    for i in range(3):
        c = slice(i * width, (i + 1) * width)
        copies[1 + i].wait()
        picked = lax.dot_general(
            onehot, x_ref[i], (((0,), (0,)), ((), ())), preferred_element_type=jnp.float32
        )
        out_ref[:, :, c] = picked.reshape(out_ref.shape[0], out_ref.shape[1], width).astype(
            jnp.bfloat16
        )
        outs.append(
            pltpu.make_async_copy(out_ref.at[:, :, c], out_hbm.at[:, :, c], out_sems.at[i])
        )
        outs[-1].start()
    for copy in outs:
        copy.wait()


def attend(q, k, v, masks, head, row_block, column_block):
    depth = q.shape[1]
    scores = lax.dot_general(q, k, (((1,), (1,)), ((), ())), preferred_element_type=jnp.float32)
    scores = scores * (1.0 / math.sqrt(depth))
    seen = [masks[4 * head + i] for i in range(4)]
    chosen = jnp.where(
        row_block == 0,
        jnp.where(column_block == 0, seen[0], seen[1]),
        jnp.where(column_block == 0, seen[2], seen[3]),
    )
    visible = chosen == 1
    scores = jnp.where(visible, scores, -jnp.inf)
    row_max = jnp.max(scores, axis=1, keepdims=True)
    weights = jnp.exp(scores - row_max)
    total = jnp.sum(weights, axis=1, keepdims=True)
    combined = jnp.dot(weights.astype(jnp.bfloat16), v, preferred_element_type=jnp.float32)
    return combined / total


def near_kernel(masks_ref, q_ref, k_ref, v_ref, out_ref):
    rows, width = q_ref.shape
    heads = masks_ref.shape[0] // 4
    depth = width // heads
    row_block = lax.broadcasted_iota(jnp.int32, (rows, rows), 0) // (rows // 2)
    column_block = lax.broadcasted_iota(jnp.int32, (rows, rows), 1) // (rows // 2)
    for h in range(heads):
        c = slice(h * depth, (h + 1) * depth)
        out_ref[:, c] = attend(
            q_ref[:, c], k_ref[:, c], v_ref[:, c], masks_ref, h, row_block, column_block
        ).astype(jnp.bfloat16)


def quarter_of(core, y, z):
    return jnp.where(core == 0, z + 2 * y, 2 * z + y) % 4


def message_kernel(w_ref, out_ref):
    core = lax.rem(lax.axis_index("mlp"), 2)
    place, row = iotas((256, w_ref.shape[0]))
    first = 12 * quarter_of(core, place // 64, place // 16 % 4)
    pick = ones_where((place % 16 >= 4) & (row == first + place % 16 - 4))
    got = jnp.dot(pick, w_ref[...], preferred_element_type=jnp.float32)
    out_ref[...] = got.reshape(out_ref.shape).astype(jnp.bfloat16)


def far_kernel(masks_ref, x_ref, weights_ref, after_hbm, out_ref):
    frames, group, wide = x_ref.shape
    rows, width = frames * group, wide // 3
    heads = masks_ref.shape[0] // 4
    row, column = iotas((rows, rows))
    row_block, column_block = row % group // (group // 2), column % group // (group // 2)
    at, row = iotas((8 * frames, rows))
    spread = ones_where((at % 8 < group) & (at // 8 * group + at % 8 == row))
    outs = []
    for h in range(heads):
        q, k, v = (
            x_ref[:, :, i * width + h * LANES : i * width + (h + 1) * LANES]
            .astype(jnp.float32)
            .reshape(rows, LANES)
            .astype(jnp.bfloat16)
            for i in range(3)
        )
        out = attend(q, k, v, masks_ref, h, row_block, column_block)
        outs.append(out.astype(jnp.bfloat16))
    out = jnp.dot(spread, jnp.concatenate(outs, axis=1), preferred_element_type=jnp.float32)
    weights = weights_ref[...].astype(jnp.float32).reshape(1, 4, 1, 4, 16, width)
    first = out.reshape(2, 4, 2, 4, 8, width) + weights[:, :, :, :, :8]
    rest = jnp.broadcast_to(weights[:, :, :, :, 8:], first.shape)
    message = jnp.concatenate(
        [first.reshape(frames, 8, width), rest.reshape(frames, 8, width)], axis=1
    )
    out_ref[...] = message.astype(jnp.bfloat16)


def select_kernel(
    kinds_ref, order_ref, far_ref, near_ref, out_hbm, own_ref, out_ref, sems
):
    rows, width = near_ref.shape
    heads = kinds_ref.shape[0]
    onehot = placement(order_ref[...], rows)
    far = far_ref[...].astype(jnp.float32)[:, :4].reshape(rows, width).astype(jnp.bfloat16)
    copies = []
    for half in range(2):
        r = slice(half * rows // 2, (half + 1) * rows // 2)
        back = jnp.dot(onehot[r], far, preferred_element_type=jnp.float32)
        near = near_ref[r, :].astype(jnp.float32)
        chosen = []
        for h in range(heads):
            c = slice(h * LANES, (h + 1) * LANES)
            chosen.append(jnp.where(kinds_ref[h] == 1, back[:, c], near[:, c]).astype(jnp.bfloat16))
        out_ref[r, :] = jnp.concatenate(chosen, axis=1)
        for x in range(out_hbm.shape[0]):
            copies.append(
                pltpu.make_async_copy(out_ref.at[r], out_hbm.at[x, r], sems.at[2 * x + half])
            )
            copies[-1].start()
    n, part = own_ref.shape[:2]
    row, at = iotas((part, 16 * n))
    take = ones_where(row // 12 * 16 + 4 + row % 12 == at)
    for y in range(n):
        block = far_ref[y * n : (y + 1) * n].astype(jnp.float32).reshape(16 * n, width)
        got = jnp.dot(take, block.astype(jnp.bfloat16), preferred_element_type=jnp.float32)
        own_ref[y] = got.astype(jnp.bfloat16)
    for copy in copies:
        copy.wait()


def order_kernel(x_ref, out_ref):
    width = x_ref.shape[2]
    place = lax.broadcasted_iota(jnp.int32, (1, width), 1)
    quarter = sum((place >= edge).astype(jnp.int32) for edge in (96, 192, 288))
    left = place - 96 * quarter
    z = sum((left >= 12 * i).astype(jnp.int32) for i in range(1, 8))
    column = 48 * z + 12 * quarter + left - 12 * z
    old = lax.broadcasted_iota(jnp.int32, (width, width), 0)
    to_weight = ones_where(old == column)
    for x in range(x_ref.shape[0]):
        out_ref[x] = jnp.dot(x_ref[x], to_weight, preferred_element_type=jnp.float32).astype(
            jnp.bfloat16
        )


def weight_kernel(own_ref, next_ref, last_ref, second_ref, out_ref):
    seq = lax.axis_index("seq")
    quarter = quarter_of(lax.rem(lax.axis_index("mlp"), 2), seq // 8, lax.rem(seq, 8))
    part = own_ref.shape[1]
    for step, ref in ((0, own_ref), (1, next_ref), (3, last_ref), (2, second_ref)):
        rows = pl.ds(pl.multiple_of(lax.rem(quarter + step, 4) * part, part), part)
        out_ref[:, rows, :] = ref[...]


def project_kernel(gate_ref, x_ref, others_ref, w_ref, out_ref):
    core = lax.rem(lax.axis_index("mlp"), 2)
    total = None
    for ref, parity in ((x_ref, core), (others_ref, 1 - core)):
        for x in range(0, x_ref.shape[0], 2):
            heads = jnp.concatenate([ref[x], ref[x + 1]], axis=1)
            weight = jnp.concatenate([w_ref[2 * x + parity], w_ref[2 * x + 2 + parity]], axis=0)
            got = jnp.dot(heads, weight, preferred_element_type=jnp.float32)
            total = got if total is None else total + got
    out_ref[...] = (gate_ref[...] * total).astype(jnp.bfloat16)


def call(kernel, shape, specs, *args, out=VMEM, scratch=(), limit=16, cost=None):
    shapes = shape if isinstance(shape, list) else [shape]
    shapes = [jax.ShapeDtypeStruct(one, jnp.bfloat16) for one in shapes]
    return pl.pallas_call(
        kernel,
        out_shape=shapes if isinstance(shape, list) else shapes[0],
        in_specs=specs,
        out_specs=out,
        scratch_shapes=scratch,
        compiler_params=pltpu.CompilerParams(vmem_limit_bytes=limit * 1024 * 1024),
        cost_estimate=cost,
    )(*args)


def fetch(block, offsets):
    pairs = []
    for y in range(8):
        for z in range(8):
            for m in range(8):
                dy, dz = offsets[m % 2]
                source = (y + dy) % 8 * 8 + (z + dz) % 8
                pairs.append((8 * source + m, 8 * (8 * y + z) + m))
    return lax.ppermute(block, ("seq", "mlp"), pairs)


def local(
    queries, key_vectors, value_vectors, head_kinds, block_masks, order_map, out_weight, gate_values
):
    rows, width = queries.shape
    frames = lax.axis_size("seq")
    parts = lax.axis_size("mlp")
    group = rows // frames
    masks = block_masks.reshape(-1)
    order = order_map.reshape(1, rows)
    sent = call(
        send_kernel,
        (frames, group, 3 * width),
        [HBM] * 4,
        order,
        queries,
        key_vectors,
        value_vectors,
        scratch=[
            pltpu.VMEM((1, rows), jnp.int32),
            pltpu.VMEM((3, rows, width), jnp.bfloat16),
            pltpu.VMEM((frames, group, 3 * width), jnp.bfloat16),
            pltpu.SemaphoreType.DMA((4,)),
            pltpu.SemaphoreType.DMA((3,)),
        ],
        out=HBM,
        limit=60,
    )
    moved = lax.all_to_all(sent, "seq", split_axis=0, concat_axis=0, tiled=True)
    near = call(near_kernel, (rows, width), [SMEM] + [VMEM] * 3, masks, queries, key_vectors, value_vectors)
    pieces = call(message_kernel, (16, 16, width), [VMEM], out_weight)
    far = call(
        far_kernel, (frames, 16, width), [SMEM, VMEM, VMEM, HBM], masks, moved, pieces, near
    )
    returned = lax.all_to_all(far, "seq", split_axis=0, concat_axis=0, tiled=True)

    attended, own = call(
        select_kernel,
        [(parts // 2, rows, width), (parts, 96, width)],
        [SMEM] + [VMEM] * 3,
        head_kinds,
        order,
        returned,
        near,
        out=[HBM, VMEM],
        scratch=[pltpu.VMEM((rows, width), jnp.bfloat16), pltpu.SemaphoreType.DMA((parts,))],
    )
    others = [
        fetch(own, offsets) for offsets in (((0, 1), (1, 0)), ((0, -1), (-1, 0)), ((1, 0), (0, 1)))
    ]
    columns = lax.all_to_all(
        attended,
        "mlp",
        split_axis=0,
        concat_axis=0,
        axis_index_groups=[[0, 2, 4, 6], [1, 3, 5, 7]],
        tiled=True,
    )
    columns = call(order_kernel, (parts // 2, rows, width), [VMEM], columns)
    others_columns = lax.ppermute(columns, "mlp", [(i, i ^ 1) for i in range(parts)])
    weight = call(
        weight_kernel,
        (parts, width, width),
        [VMEM] * 4,
        own,
        *others,
        cost=pl.CostEstimate(flops=COST, bytes_accessed=0, transcendentals=0),
    )
    return call(
        project_kernel,
        (rows, width),
        [VMEM] * 4,
        gate_values.reshape(1, width),
        columns,
        others_columns,
        weight,
    )


def solution(mesh):
    in_specs = (
        P("seq", "mlp"),
        P("seq", "mlp"),
        P("seq", "mlp"),
        P("mlp"),
        P("mlp", None, None),
        P(),
        P("seq", "mlp"),
        P("mlp"),
    )
    out_specs = P("seq", "mlp")
    return jax.shard_map(local, mesh=mesh, in_specs=in_specs, out_specs=out_specs, check_vma=False)
```

```python
import math

import jax
import jax.numpy as jnp
from jax import lax
from jax.experimental import pallas as pl
from jax.experimental.pallas import tpu as pltpu
from jax.sharding import PartitionSpec as P

HBM = pl.BlockSpec(memory_space=pltpu.HBM)
VMEM = pl.BlockSpec(memory_space=pltpu.VMEM)
LANES = 128
COST = 20 * 10**9
SMEM = pl.BlockSpec(memory_space=pltpu.SMEM)


def placement(order, rows):
    positions = lax.broadcasted_iota(jnp.int32, (rows, rows), 0)
    return (positions == order).astype(jnp.float32).astype(jnp.bfloat16)


def ones_where(condition):
    return condition.astype(jnp.float32).astype(jnp.bfloat16)


def iotas(shape):
    return lax.broadcasted_iota(jnp.int32, shape, 0), lax.broadcasted_iota(jnp.int32, shape, 1)


def send_kernel(
    order_hbm, q_hbm, k_hbm, v_hbm, out_hbm, order_ref, x_ref, out_ref, sems, out_sems
):
    pairs = [(order_hbm, order_ref)]
    pairs += [(src, x_ref.at[i]) for i, src in enumerate((q_hbm, k_hbm, v_hbm))]
    copies = [pltpu.make_async_copy(src, dst, sems.at[i]) for i, (src, dst) in enumerate(pairs)]
    for copy in copies:
        copy.start()
    rows, width = x_ref.shape[1:]
    copies[0].wait()
    onehot = placement(order_ref[...], rows)
    outs = []
    for i in range(3):
        c = slice(i * width, (i + 1) * width)
        copies[1 + i].wait()
        picked = lax.dot_general(
            onehot, x_ref[i], (((0,), (0,)), ((), ())), preferred_element_type=jnp.float32
        )
        out_ref[:, :, c] = picked.reshape(out_ref.shape[0], out_ref.shape[1], width).astype(
            jnp.bfloat16
        )
        outs.append(
            pltpu.make_async_copy(out_ref.at[:, :, c], out_hbm.at[:, :, c], out_sems.at[i])
        )
        outs[-1].start()
    for copy in outs:
        copy.wait()


def attend(q, k, v, masks, head, row_block, column_block):
    depth = q.shape[1]
    scores = lax.dot_general(q, k, (((1,), (1,)), ((), ())), preferred_element_type=jnp.float32)
    scores = scores * (1.0 / math.sqrt(depth))
    seen = [masks[4 * head + i] for i in range(4)]
    chosen = jnp.where(
        row_block == 0,
        jnp.where(column_block == 0, seen[0], seen[1]),
        jnp.where(column_block == 0, seen[2], seen[3]),
    )
    visible = chosen == 1
    scores = jnp.where(visible, scores, -jnp.inf)
    row_max = jnp.max(scores, axis=1, keepdims=True)
    weights = jnp.exp(scores - row_max)
    total = jnp.sum(weights, axis=1, keepdims=True)
    combined = jnp.dot(weights.astype(jnp.bfloat16), v, preferred_element_type=jnp.float32)
    return combined / total


def near_kernel(masks_ref, q_ref, k_ref, v_ref, out_ref):
    rows, width = q_ref.shape
    heads = masks_ref.shape[0] // 4
    depth = width // heads
    row_block = lax.broadcasted_iota(jnp.int32, (rows, rows), 0) // (rows // 2)
    column_block = lax.broadcasted_iota(jnp.int32, (rows, rows), 1) // (rows // 2)
    for h in range(heads):
        c = slice(h * depth, (h + 1) * depth)
        out_ref[:, c] = attend(
            q_ref[:, c], k_ref[:, c], v_ref[:, c], masks_ref, h, row_block, column_block
        ).astype(jnp.bfloat16)


def quarter_of(core, y, z):
    return jnp.where(core == 0, z + 2 * y, 2 * z + y) % 4


def message_kernel(w_ref, out_ref):
    core = lax.rem(lax.axis_index("mlp"), 2)
    place, row = iotas((256, w_ref.shape[0]))
    first = 12 * quarter_of(core, place // 64, place // 16 % 4)
    pick = ones_where((place % 16 >= 4) & (row == first + place % 16 - 4))
    got = jnp.dot(pick, w_ref[...], preferred_element_type=jnp.float32)
    out_ref[...] = got.reshape(out_ref.shape).astype(jnp.bfloat16)


def far_kernel(masks_ref, x_ref, weights_ref, after_hbm, out_ref):
    frames, group, wide = x_ref.shape
    rows, width = frames * group, wide // 3
    heads = masks_ref.shape[0] // 4
    row, column = iotas((rows, rows))
    row_block, column_block = row % group // (group // 2), column % group // (group // 2)
    at, row = iotas((8 * frames, rows))
    spread = ones_where((at % 8 < group) & (at // 8 * group + at % 8 == row))
    outs = []
    for h in range(heads):
        q, k, v = (
            x_ref[:, :, i * width + h * LANES : i * width + (h + 1) * LANES]
            .astype(jnp.float32)
            .reshape(rows, LANES)
            .astype(jnp.bfloat16)
            for i in range(3)
        )
        out = attend(q, k, v, masks_ref, h, row_block, column_block)
        outs.append(out.astype(jnp.bfloat16))
    out = jnp.dot(spread, jnp.concatenate(outs, axis=1), preferred_element_type=jnp.float32)
    weights = weights_ref[...].astype(jnp.float32).reshape(1, 4, 1, 4, 16, width)
    first = out.reshape(2, 4, 2, 4, 8, width) + weights[:, :, :, :, :8]
    rest = jnp.broadcast_to(weights[:, :, :, :, 8:], first.shape)
    message = jnp.concatenate(
        [first.reshape(frames, 8, width), rest.reshape(frames, 8, width)], axis=1
    )
    out_ref[...] = message.astype(jnp.bfloat16)


def select_kernel(
    kinds_ref, order_ref, far_ref, near_ref, out_hbm, own_ref, out_ref, sems
):
    rows, width = near_ref.shape
    heads = kinds_ref.shape[0]
    onehot = placement(order_ref[...], rows)
    far = far_ref[...].astype(jnp.float32)[:, :4].reshape(rows, width).astype(jnp.bfloat16)
    copies = []
    for step in range(4):
        r = slice(step * rows // 4, (step + 1) * rows // 4)
        back = jnp.dot(onehot[r], far, preferred_element_type=jnp.float32)
        near = near_ref[r, :].astype(jnp.float32)
        chosen = []
        for h in range(heads):
            c = slice(h * LANES, (h + 1) * LANES)
            chosen.append(jnp.where(kinds_ref[h] == 1, back[:, c], near[:, c]).astype(jnp.bfloat16))
        out_ref[r, :] = jnp.concatenate(chosen, axis=1)
        for x in range(out_hbm.shape[0]):
            copies.append(
                pltpu.make_async_copy(out_ref.at[r], out_hbm.at[x, r], sems.at[4 * x + step])
            )
            copies[-1].start()
    n, part = own_ref.shape[:2]
    row, at = iotas((part, 16 * n))
    take = ones_where(row // 12 * 16 + 4 + row % 12 == at)
    for y in range(n):
        block = far_ref[y * n : (y + 1) * n].astype(jnp.float32).reshape(16 * n, width)
        got = jnp.dot(take, block.astype(jnp.bfloat16), preferred_element_type=jnp.float32)
        own_ref[y] = got.astype(jnp.bfloat16)
    for copy in copies:
        copy.wait()


def order_kernel(x_ref, out_ref):
    width = x_ref.shape[2]
    place = lax.broadcasted_iota(jnp.int32, (1, width), 1)
    quarter = sum((place >= edge).astype(jnp.int32) for edge in (96, 192, 288))
    left = place - 96 * quarter
    z = sum((left >= 12 * i).astype(jnp.int32) for i in range(1, 8))
    column = 48 * z + 12 * quarter + left - 12 * z
    old = lax.broadcasted_iota(jnp.int32, (width, width), 0)
    to_weight = ones_where(old == column)
    for x in range(x_ref.shape[0]):
        out_ref[x] = jnp.dot(x_ref[x], to_weight, preferred_element_type=jnp.float32).astype(
            jnp.bfloat16
        )


def weight_kernel(own_ref, next_ref, last_ref, second_ref, out_ref):
    seq = lax.axis_index("seq")
    quarter = quarter_of(lax.rem(lax.axis_index("mlp"), 2), seq // 8, lax.rem(seq, 8))
    part = own_ref.shape[1]
    for step, ref in ((0, own_ref), (1, next_ref), (3, last_ref), (2, second_ref)):
        rows = pl.ds(pl.multiple_of(lax.rem(quarter + step, 4) * part, part), part)
        out_ref[:, rows, :] = ref[...]


def project_kernel(gate_ref, x_ref, others_ref, w_ref, out_ref):
    core = lax.rem(lax.axis_index("mlp"), 2)
    total = None
    for ref, parity in ((x_ref, core), (others_ref, 1 - core)):
        for x in range(0, x_ref.shape[0], 2):
            heads = jnp.concatenate([ref[x], ref[x + 1]], axis=1)
            weight = jnp.concatenate([w_ref[2 * x + parity], w_ref[2 * x + 2 + parity]], axis=0)
            got = jnp.dot(heads, weight, preferred_element_type=jnp.float32)
            total = got if total is None else total + got
    out_ref[...] = (gate_ref[...] * total).astype(jnp.bfloat16)


def call(kernel, shape, specs, *args, out=VMEM, scratch=(), limit=16, cost=None):
    shapes = shape if isinstance(shape, list) else [shape]
    shapes = [jax.ShapeDtypeStruct(one, jnp.bfloat16) for one in shapes]
    return pl.pallas_call(
        kernel,
        out_shape=shapes if isinstance(shape, list) else shapes[0],
        in_specs=specs,
        out_specs=out,
        scratch_shapes=scratch,
        compiler_params=pltpu.CompilerParams(vmem_limit_bytes=limit * 1024 * 1024),
        cost_estimate=cost,
    )(*args)


def fetch(block, offsets):
    pairs = []
    for y in range(8):
        for z in range(8):
            for m in range(8):
                dy, dz = offsets[m % 2]
                source = (y + dy) % 8 * 8 + (z + dz) % 8
                pairs.append((8 * source + m, 8 * (8 * y + z) + m))
    return lax.ppermute(block, ("seq", "mlp"), pairs)


def local(
    queries, key_vectors, value_vectors, head_kinds, block_masks, order_map, out_weight, gate_values
):
    rows, width = queries.shape
    frames = lax.axis_size("seq")
    parts = lax.axis_size("mlp")
    group = rows // frames
    masks = block_masks.reshape(-1)
    order = order_map.reshape(1, rows)
    sent = call(
        send_kernel,
        (frames, group, 3 * width),
        [HBM] * 4,
        order,
        queries,
        key_vectors,
        value_vectors,
        scratch=[
            pltpu.VMEM((1, rows), jnp.int32),
            pltpu.VMEM((3, rows, width), jnp.bfloat16),
            pltpu.VMEM((frames, group, 3 * width), jnp.bfloat16),
            pltpu.SemaphoreType.DMA((4,)),
            pltpu.SemaphoreType.DMA((3,)),
        ],
        out=HBM,
        limit=60,
    )
    moved = lax.all_to_all(sent, "seq", split_axis=0, concat_axis=0, tiled=True)
    near = call(near_kernel, (rows, width), [SMEM] + [VMEM] * 3, masks, queries, key_vectors, value_vectors)
    pieces = call(message_kernel, (16, 16, width), [VMEM], out_weight)
    far = call(
        far_kernel, (frames, 16, width), [SMEM, VMEM, VMEM, HBM], masks, moved, pieces, near
    )
    returned = lax.all_to_all(far, "seq", split_axis=0, concat_axis=0, tiled=True)

    attended, own = call(
        select_kernel,
        [(parts // 2, rows, width), (parts, 96, width)],
        [SMEM] + [VMEM] * 3,
        head_kinds,
        order,
        returned,
        near,
        out=[HBM, VMEM],
        scratch=[pltpu.VMEM((rows, width), jnp.bfloat16), pltpu.SemaphoreType.DMA((2 * parts,))],
    )
    others = [
        fetch(own, offsets) for offsets in (((0, 1), (1, 0)), ((0, -1), (-1, 0)), ((1, 0), (0, 1)))
    ]
    columns = lax.all_to_all(
        attended,
        "mlp",
        split_axis=0,
        concat_axis=0,
        axis_index_groups=[[0, 2, 4, 6], [1, 3, 5, 7]],
        tiled=True,
    )
    columns = call(order_kernel, (parts // 2, rows, width), [VMEM], columns)
    others_columns = lax.ppermute(columns, "mlp", [(i, i ^ 1) for i in range(parts)])
    weight = call(
        weight_kernel,
        (parts, width, width),
        [VMEM] * 4,
        own,
        *others,
        cost=pl.CostEstimate(flops=COST, bytes_accessed=0, transcendentals=0),
    )
    return call(
        project_kernel,
        (rows, width),
        [VMEM] * 4,
        gate_values.reshape(1, width),
        columns,
        others_columns,
        weight,
    )


def solution(mesh):
    in_specs = (
        P("seq", "mlp"),
        P("seq", "mlp"),
        P("seq", "mlp"),
        P("mlp"),
        P("mlp", None, None),
        P(),
        P("seq", "mlp"),
        P("mlp"),
    )
    out_specs = P("seq", "mlp")
    return jax.shard_map(local, mesh=mesh, in_specs=in_specs, out_specs=out_specs, check_vma=False)
```
